32 devices in a mesh: gy: 4 (over y, x), gx: 8 (over z, core).
Axes of the slice: x: 2, y: 2, z: 4, core: 2. Of those that a mesh axis runs over, the one named last changes fastest.
Arguments:
- estimate: float32 [128, 128, 128], P('gy', 'gx'), may hold values from 0.5 to 2
- recorded: float32 [4, 128, 128, 128], P(None, 'gy', 'gx'), may hold values from 0.2 to 5
- quarter_turns: int32 [4], replicated, may hold values from 0 to 3, each once
- offsets: int32 [4], replicated, may hold values from 0 to 127
- depth_taps: float32 [4, 41], replicated, may hold values from 0.002 to 0.1
- row_taps: float32 [4, 9], replicated, may hold values from 0.01 to 0.5
- column_taps: float32 [4, 9], replicated, may hold values from 0.01 to 0.5
Outputs:
- deconvolved: float32 [128, 128, 128], P('gy', 'gx')
The draws below stay inside these ranges and needn't reach their ends.
Inputs may be any that keep to these rules, and one draw needn't show every extreme that they name: `quarter_turns`: every view has a different number of quarter turns.
All inputs are finite; a program needn't handle non-finite values.
Results may differ from the reference program's by a relative error of at most 0.0001.
Values sent between devices are 32-bit elements; how exact they have to be, the bound alone decides.
No kernel may reach another device: no remote copies, remote signals or barrier semaphores. Data moves between devices by JAX's collectives and lax.ppermute only.
A program may use at most 128 MiB of HBM per device.

```python
import math
import jax
import jax.numpy as jnp
from jax import lax

VIEWS = 4
KZ = 41
KS = 9
ITERS = 1
Z = 128
N = 128


def with_ends(values, own_key, least, largest):
    index_at = [jax.random.randint(jax.random.fold_in(own_key, axis), (), 0, length) for axis, length in enumerate(values.shape)]
    main_axis = values.shape.index(max(values.shape))
    next_to = index_at[:main_axis] + [(index_at[main_axis] + 1) % values.shape[main_axis]] + index_at[main_axis + 1:]
    return values.at[tuple(index_at)].set(least).at[tuple(next_to)].set(largest)


def levels(rng, extent, cuts, low, high):
    def one(position, shards_of):
        steps = jax.random.uniform(jax.random.fold_in(jax.random.fold_in(rng, 6), position), (shards_of,), jnp.float32, low / len(cuts), high / len(cuts))
        return jnp.repeat(jnp.exp(steps), extent[position] // shards_of).reshape((-1,) + (1,) * (len(extent) - position - 1))

    factor_of = one(*cuts[0])
    for cut in cuts[1:]:
        factor_of = factor_of * one(*cut)
    return factor_of


def setup_inputs(seed: int = 0) -> dict:
    key_of = jax.random.split(jax.random.key(seed), 8)
    return {
        "estimate": jnp.clip(jnp.exp(math.log(2.0) - 1.3862944 * jax.random.uniform(key_of[0], (Z, N, N), jnp.float32) ** levels(key_of[0], (Z, N, N), ((0, 4), (1, 8)), -0.2, 0.2)), 0.5, 2.0),
        "recorded": jnp.clip(jnp.exp(math.log(5.0) - 3.218876 * jax.random.uniform(key_of[1], (VIEWS, Z, N, N), jnp.float32) ** levels(key_of[1], (VIEWS, Z, N, N), ((1, 4), (2, 8)), -0.2, 0.2)), 0.2, 5.0),
        "quarter_turns": jax.random.permutation(key_of[2], 4).astype(jnp.int32),
        "offsets": with_ends(jax.random.randint(key_of[3], (VIEWS,), 0, N), jax.random.fold_in(key_of[3], 1), 0, N - 1).astype(jnp.int32),
        "depth_taps": jnp.clip(jnp.exp(jax.random.uniform(key_of[4], (VIEWS, KZ), jnp.float32, math.log(0.002), math.log(0.1))), 0.002, 0.1),
        "row_taps": jnp.clip(jnp.exp(jax.random.uniform(key_of[5], (VIEWS, KS), jnp.float32, math.log(0.01), math.log(0.5))), 0.01, 0.5),
        "column_taps": jnp.clip(jnp.exp(jax.random.uniform(key_of[6], (VIEWS, KS), jnp.float32, math.log(0.01), math.log(0.5))), 0.01, 0.5),
    }


def band_matrix(taps, length):
    width = taps.shape[0]
    offset = jnp.arange(length + width - 1)[None, :] - jnp.arange(length)[:, None]
    inside = (offset >= 0) & (offset < width)
    return jnp.where(inside, taps[jnp.clip(offset, 0, width - 1)], jnp.zeros((), taps.dtype))


def blur_volume(volume, depth_row, first_row, last_row):
    depth_half = (depth_row.shape[0] - 1) // 2
    side_half = (first_row.shape[0] - 1) // 2
    padded = jnp.pad(volume, ((depth_half, depth_half), (0, 0), (0, 0)))
    result = jnp.einsum("ik,ksl->isl", band_matrix(depth_row, volume.shape[0]), padded, precision=lax.Precision.HIGHEST)
    padded = jnp.pad(result, ((0, 0), (side_half, side_half), (0, 0)))
    result = jnp.einsum("jk,ikl->ijl", band_matrix(first_row, volume.shape[1]), padded, precision=lax.Precision.HIGHEST)
    padded = jnp.pad(result, ((0, 0), (0, 0), (side_half, side_half)))
    return jnp.einsum("ijk,lk->ijl", padded, band_matrix(last_row, volume.shape[2]), precision=lax.Precision.HIGHEST)


def rotate_once(volume):
    return jnp.flip(jnp.swapaxes(volume, 1, 2), axis=2)


def rotate(volume, turns_now):
    return lax.fori_loop(0, turns_now, lambda unused, inner: rotate_once(inner), volume)


def reference(estimate, recorded, quarter_turns, offsets, depth_taps, row_taps, column_taps):
    current = estimate
    for iteration in range(ITERS):
        total = jnp.zeros_like(current)
        for view_index in range(VIEWS):
            turns_now = quarter_turns[view_index]
            shift_now = offsets[view_index]
            seen = rotate(current, turns_now)
            blurred = blur_volume(seen, depth_taps[view_index], row_taps[view_index], column_taps[view_index])
            predicted = jnp.roll(blurred, shift_now, axis=2)
            ratio = recorded[view_index] / predicted
            unrolled = jnp.roll(ratio, -shift_now, axis=2)
            backed = blur_volume(unrolled, depth_taps[view_index][::-1], row_taps[view_index][::-1], column_taps[view_index][::-1])
            total = total + rotate(backed, (4 - turns_now) % 4)
        current = current * total / VIEWS
    return current
```

```python
import functools

import jax
import jax.numpy as jnp
from jax import lax
from jax.experimental import pallas as pl
from jax.experimental.pallas import tpu as pltpu
from jax.sharding import PartitionSpec as P

VIEWS = 4
LANES = 128
VMEM = pl.BlockSpec(memory_space=pltpu.VMEM)
SMEM = pl.BlockSpec(memory_space=pltpu.SMEM)
PARAMS = pltpu.CompilerParams(vmem_limit_bytes=24 * 1024 * 1024)
F32 = jnp.float32
BF16 = jnp.bfloat16


def struct(*shape, dtype=F32):
    return jax.ShapeDtypeStruct(shape, dtype)


def view_of(turns_ref, turn):
    found = jnp.int32(0)
    for view in range(1, VIEWS):
        found = jnp.where(turns_ref[view] == turn, jnp.int32(view), found)
    return found


def split(value):
    high = value.astype(BF16)
    return high, (value - high.astype(F32)).astype(BF16)


def dot(left, right):
    return jnp.dot(left, right, preferred_element_type=F32)


def along(axis, width):
    return [(i, i + 1) for i in range(width - 1)], [(i + 1, i) for i in range(width - 1)]


def prepare(turns, offsets, recorded, kept, mirrored, sent):
    depth, rows, lanes = recorded.shape[1:]
    parts = sent.shape[0]
    kept[...] = recorded[view_of(turns, 0)]
    mirrored[...] = recorded[view_of(turns, 2)]
    for slot, turn in enumerate((1, 3)):
        view = view_of(turns, turn)
        volume = recorded[view].reshape(depth * rows, lanes)
        volume = pltpu.roll(volume, lax.rem(lanes - offsets[view], lanes), 1)
        across = volume.T
        for part in range(parts):
            to = parts - 1 - part if turn == 1 else part
            sent[to, slot] = across[part * rows : (part + 1) * rows]


def edges(own, before, after, left, right):
    depth, rows, _ = own.shape
    reach = before.shape[0]
    side = left.shape[0]
    for target, initial in ((left, 0), (right, rows - side)):
        for i in range(side):
            target[i, 0:depth] = own[:, initial + i]
            target[i, depth : depth + reach] = before[:, initial + i]
            target[i, depth + reach : depth + 2 * reach] = after[:, initial + i]


def row_taps_of(turn, view, row_taps, column_taps, width):
    source = column_taps if turn % 2 else row_taps
    flipped = turn in (1, 2)
    return [source[view, width - 1 - s if flipped else s] for s in range(width)]


def predict(turns, offsets, depth_taps, row_taps, column_taps, own, before, after, left, right,
            predicted, lane_back, depth_back, extended, blurred):
    depth, rows, lanes = own.shape
    reach = before.shape[0]
    side = left.shape[0]
    width = 2 * side + 1
    deep = depth + 2 * reach
    padded = extended.shape[1]
    views = [view_of(turns, turn) for turn in range(VIEWS)]

    column = lax.broadcasted_iota(jnp.int32, (depth, LANES), 1)
    row = lax.broadcasted_iota(jnp.int32, (depth, LANES), 0)
    layer = jnp.where(column < depth, column, jnp.where(column < depth + reach, column - depth - reach, column - reach))
    tap = jnp.where(column < deep, layer - row + reach, -1)
    stacked = []
    for view in views:
        matrix = jnp.zeros((depth, LANES), F32)
        for t in range(2 * reach + 1):
            matrix = jnp.where(tap == t, depth_taps[view, t], matrix)
        stacked.append(matrix)
    matrix = jnp.concatenate(stacked, axis=0)
    back_high, back_low = split(matrix.T[:padded])
    depth_back[0] = back_high
    depth_back[1] = back_low
    high, low = split(matrix)
    zero = jnp.zeros((VIEWS * depth, LANES - padded), BF16)
    del zero
    depth_high, depth_low = high[:, :padded], low[:, :padded]

    for i in range(side):
        extended[i, 0:deep] = left[i]
        extended[side + rows + i, 0:deep] = right[i]
    for i in range(rows):
        extended[side + i, 0:depth] = own[:, i]
        extended[side + i, depth : depth + reach] = before[:, i]
        extended[side + i, depth + reach : deep] = after[:, i]
    if padded > deep:
        for i in range(rows + 2 * side):
            extended[i, deep:padded] = jnp.zeros((padded - deep, lanes), F32)

    for i in range(rows + 2 * side):
        e_high, e_low = split(extended[i])
        blurred[i] = dot(depth_high, e_high) + dot(depth_high, e_low) + dot(depth_low, e_high)

    inward = lax.broadcasted_iota(jnp.int32, (lanes, lanes), 0)
    outward = lax.broadcasted_iota(jnp.int32, (lanes, lanes), 1)
    for turn, view in enumerate(views):
        place = outward
        if turn % 2 == 0:
            place = outward - offsets[view]
            place = jnp.where(place < 0, place + lanes, place)
        tap = (lanes - 1 - place - inward if turn >= 2 else inward - place) + side
        source = row_taps if turn % 2 else column_taps
        matrix = jnp.zeros((lanes, lanes), F32)
        for r in range(width):
            matrix = jnp.where(tap == r, source[view, r], matrix)
        high, low = split(matrix)
        back_high, back_low = split(matrix.T)
        lane_back[turn, 0] = back_high
        lane_back[turn, 1] = back_low
        both = jnp.concatenate([high, high], axis=0)
        factor = row_taps_of(turn, view, row_taps, column_taps, width)
        for i in range(rows):
            layers = pl.ds(turn * depth, depth)
            total = factor[0] * blurred[i, layers]
            for s in range(1, width):
                total = total + factor[s] * blurred[i + s, layers]
            t_high, t_low = split(total)
            predicted[turn, i] = dot(jnp.concatenate([t_high, t_low], axis=1), both) + dot(t_high, low)


def project(turns, row_taps, column_taps, predicted, lane_back, depth_back, kept, mirrored, arrived,
            middle, left, right, data, backed, spread):
    _, rows, depth, lanes = predicted.shape
    side = left.shape[0]
    deep = left.shape[1]
    width = 2 * side + 1
    views = [view_of(turns, turn) for turn in range(VIEWS)]
    parts = arrived.shape[0]
    group = LANES // rows
    granule = lax.broadcasted_iota(jnp.int32, (8, LANES), 1) // rows

    for slot in range(2):
        for part in range(0, parts, group):
            for eight in range(0, rows, 8):
                for chunk in range(depth * rows // LANES):
                    held = [
                        arrived[part + s, slot, eight : eight + 8, chunk * LANES : (chunk + 1) * LANES]
                        for s in range(group)
                    ]
                    step = 1
                    while step < group:
                        upper = (granule // step) % 2 == 1
                        swapped = list(held)
                        for s in range(group):
                            if s & step == 0:
                                one, two = held[s], held[s + step]
                                swapped[s] = jnp.where(upper, pltpu.roll(two, step * rows, 1), one)
                                swapped[s + step] = jnp.where(upper, two, pltpu.roll(one, LANES - step * rows, 1))
                        held = swapped
                        step *= 2
                    for s in range(group):
                        data[slot, eight : eight + 8, chunk * group + s, part * rows : part * rows + LANES] = held[s]

    for turn, view in enumerate(views):
        high, low = lane_back[turn, 0], lane_back[turn, 1]
        both = jnp.concatenate([high, high], axis=0)
        for i in range(rows):
            there = rows - 1 - i if turn in (1, 2) else i
            if turn == 0:
                recorded = kept[:, there]
            elif turn == 2:
                recorded = mirrored[:, there]
            else:
                recorded = data[turn // 2, there]
            r_high, r_low = split(recorded / predicted[turn, i])
            backed[turn, i] = dot(jnp.concatenate([r_high, r_low], axis=1), both) + dot(r_high, low)
        factor = row_taps_of(turn, view, row_taps, column_taps, width)
        for e in range(rows + 2 * side):
            total = None
            for i in range(max(0, e - 2 * side), min(rows, e + 1)):
                term = factor[e - i] * backed[turn, i]
                total = term if total is None else total + term
            spread[e, turn * depth : (turn + 1) * depth] = total

    high, low = depth_back[0], depth_back[1]
    both = jnp.concatenate([high, low], axis=1)
    for e in range(rows + 2 * side):
        s_high, s_low = split(spread[e])
        result = dot(both, jnp.concatenate([s_high, s_high], axis=0)) + dot(high, s_low)
        result = result[:deep]
        if e < side:
            left[e] = result
        elif e < side + rows:
            middle[e - side] = result
        else:
            right[e - side - rows] = result


def gather_sides(middle, left, right, own, up, down):
    rows = middle.shape[0]
    side = left.shape[0]
    depth = own.shape[1]
    reach = up.shape[0] // rows
    for i in range(rows):
        value = middle[i]
        if i < side:
            value = value + left[i]
        if i >= rows - side:
            value = value + right[i - rows + side]
        own[i] = value[:depth]
        up[i * reach : (i + 1) * reach] = value[depth : depth + reach]
        down[i * reach : (i + 1) * reach] = value[depth + reach : depth + 2 * reach]


def finish(estimate, own, up, down, out):
    rows, depth, _ = own.shape
    reach = up.shape[0] // rows
    for i in range(rows):
        value = own[i]
        lane = value.shape[1]
        first = up[i * reach : (i + 1) * reach]
        last = down[i * reach : (i + 1) * reach]
        rest = jnp.zeros((depth - reach, lane), F32)
        value = value + jnp.concatenate([first, rest], axis=0) + jnp.concatenate([rest, last], axis=0)
        out[:, i] = estimate[:, i] * value * (1.0 / VIEWS)


def call(body, out_shape, specs, scratch=(), cost=None):
    return pl.pallas_call(
        body,
        out_shape=out_shape,
        in_specs=specs,
        out_specs=jax.tree.map(lambda _: VMEM, out_shape),
        scratch_shapes=scratch,
        compiler_params=PARAMS,
        cost_estimate=cost,
    )


def shards(estimate, recorded, quarter_turns, offsets, depth_taps, row_taps, column_taps):
    depth, rows, lanes = estimate.shape
    reach = (depth_taps.shape[1] - 1) // 2
    side = (row_taps.shape[1] - 1) // 2
    deep = depth + 2 * reach
    padded = -(-deep // 16) * 16
    parts = lax.axis_size("gx")
    forth_y, back_y = along("gy", lax.axis_size("gy"))
    forth_x, back_x = along("gx", parts)

    before = lax.ppermute(estimate[depth - reach :], "gy", forth_y)
    after = lax.ppermute(estimate[:reach], "gy", back_y)
    kept, mirrored, sent = call(
        prepare,
        (struct(depth, rows, lanes), struct(depth, rows, lanes), struct(parts, 2, rows, depth * rows)),
        [SMEM, SMEM, VMEM],
    )(quarter_turns, offsets, recorded)
    mirrored = lax.ppermute(mirrored, "gx", [(i, parts - 1 - i) for i in range(parts)])
    arrived = lax.all_to_all(sent, "gx", 0, 0)

    left, right = call(
        edges, (struct(side, deep, lanes), struct(side, deep, lanes)), [VMEM] * 3
    )(estimate, before, after)
    left, right = lax.ppermute(right, "gx", forth_x), lax.ppermute(left, "gx", back_x)

    predicted, lane_back, depth_back = call(
        predict,
        (
            struct(VIEWS, rows, depth, lanes),
            struct(VIEWS, 2, lanes, lanes, dtype=BF16),
            struct(2, padded, VIEWS * depth, dtype=BF16),
        ),
        [SMEM] * 5 + [VMEM] * 5,
        [
            pltpu.VMEM((rows + 2 * side, padded, lanes), F32),
            pltpu.VMEM((rows + 2 * side, VIEWS * depth, lanes), F32),
        ],
        pl.CostEstimate(flops=4_000_000_000, bytes_accessed=4_000_000, transcendentals=0),
    )(quarter_turns, offsets, depth_taps, row_taps, column_taps, estimate, before, after, left, right)

    middle, left, right = call(
        project,
        (struct(rows, deep, lanes), struct(side, deep, lanes), struct(side, deep, lanes)),
        [SMEM] * 3 + [VMEM] * 6,
        [
            pltpu.VMEM((2, rows, depth, lanes), F32),
            pltpu.VMEM((VIEWS, rows, depth, lanes), F32),
            pltpu.VMEM((rows + 2 * side, VIEWS * depth, lanes), F32),
        ],
        pl.CostEstimate(flops=4_000_000_000, bytes_accessed=4_000_000, transcendentals=0),
    )(quarter_turns, row_taps, column_taps, predicted, lane_back, depth_back, kept, mirrored, arrived)

    left, right = lax.ppermute(right, "gx", forth_x), lax.ppermute(left, "gx", back_x)
    own, up, down = call(
        gather_sides,
        (struct(rows, depth, lanes), struct(rows * reach, lanes), struct(rows * reach, lanes)),
        [VMEM] * 3,
    )(middle, left, right)
    first = lax.ppermute(down, "gy", forth_y)
    last = lax.ppermute(up, "gy", back_y)
    return call(finish, struct(depth, rows, lanes), [VMEM] * 4)(estimate, own, first, last)


def solution(mesh):
    in_specs = (P("gy", "gx", None), P(None, "gy", "gx", None), P(), P(), P(), P(), P())
    out_specs = P("gy", "gx", None)
    return jax.shard_map(shards, mesh=mesh, in_specs=in_specs, out_specs=out_specs, check_vma=False)
```

```python
import functools

import jax
import jax.numpy as jnp
from jax import lax
from jax.experimental import pallas as pl
from jax.experimental.pallas import tpu as pltpu
from jax.sharding import PartitionSpec as P

VIEWS = 4
LANES = 128
VMEM = pl.BlockSpec(memory_space=pltpu.VMEM)
SMEM = pl.BlockSpec(memory_space=pltpu.SMEM)
PARAMS = pltpu.CompilerParams(vmem_limit_bytes=24 * 1024 * 1024)
F32 = jnp.float32
BF16 = jnp.bfloat16


def struct(*shape, dtype=F32):
    return jax.ShapeDtypeStruct(shape, dtype)


def view_of(turns_ref, turn):
    found = jnp.int32(0)
    for view in range(1, VIEWS):
        found = jnp.where(turns_ref[view] == turn, jnp.int32(view), found)
    return found


def split(value):
    high = value.astype(BF16)
    return high, (value - high.astype(F32)).astype(BF16)


def dot(left, right):
    return jnp.dot(left, right, preferred_element_type=F32)


def pairs(width):
    def swaps(initial):
        return [p for i in range(initial, width - 1, 2) for p in ((i, i + 1), (i + 1, i))]

    return swaps(0), swaps(1)


def is_odd(axis):
    return lax.rem(lax.axis_index(axis), 2) == 1


def prepare(turns, offsets, recorded, kept, mirrored, *rest):
    sent, across = rest[:-1], rest[-1]
    depth, rows, lanes = recorded.shape[1:]
    parts = len(sent)
    me = lax.axis_index("gx")
    kept[...] = recorded[view_of(turns, 0)]
    mirrored[...] = recorded[view_of(turns, 2)]
    for slot, turn in enumerate((1, 3)):
        view = view_of(turns, turn)
        volume = recorded[view].reshape(depth * rows, lanes)
        volume = pltpu.roll(volume, lax.rem(lanes - offsets[view], lanes), 1)
        across[...] = volume.T
        for k in range(parts):
            to = lax.bitwise_xor(me, k)
            part = parts - 1 - to if turn == 1 else to
            sent[k][slot] = across[pl.ds(pl.multiple_of(part * rows, rows), rows)]


def edges(own, even_pair, odd_pair):
    rows = own.shape[1]
    side = even_pair.shape[0]
    odd = is_odd("gx")
    for i in range(side):
        first, last = own[:, i], own[:, rows - side + i]
        even_pair[i] = jnp.where(odd, first, last)
        odd_pair[i] = jnp.where(odd, last, first)


def layers_out(own, from_even, from_odd, even_pair, odd_pair):
    depth, rows, _ = own.shape
    side = from_even.shape[0]
    reach = even_pair.shape[0] // (rows + 2 * side)
    odd_x, odd_y = is_odd("gx"), is_odd("gy")
    for e in range(rows + 2 * side):
        if e < side:
            value = jnp.where(odd_x, from_even[e], from_odd[e])
        elif e < side + rows:
            value = own[:, e - side]
        else:
            value = jnp.where(odd_x, from_odd[e - side - rows], from_even[e - side - rows])
        first, last = value[:reach], value[depth - reach :]
        even_pair[e * reach : (e + 1) * reach] = jnp.where(odd_y, first, last)
        odd_pair[e * reach : (e + 1) * reach] = jnp.where(odd_y, last, first)


def row_taps_of(turn, view, row_taps, column_taps, width):
    source = column_taps if turn % 2 else row_taps
    flipped = turn in (1, 2)
    return [source[view, width - 1 - s if flipped else s] for s in range(width)]


def predict(turns, offsets, depth_taps, row_taps, column_taps, own, even_x, odd_x, even_y, odd_y,
            predicted, lane_back, depth_back, extended, blurred):
    depth, rows, lanes = own.shape
    side = even_x.shape[0]
    reach = even_y.shape[0] // (rows + 2 * side)
    width = 2 * side + 1
    deep = depth + 2 * reach
    padded = extended.shape[1]
    views = [view_of(turns, turn) for turn in range(VIEWS)]

    column = lax.broadcasted_iota(jnp.int32, (depth, LANES), 1)
    row = lax.broadcasted_iota(jnp.int32, (depth, LANES), 0)
    layer = jnp.where(column < depth, column, jnp.where(column < depth + reach, column - depth - reach, column - reach))
    tap = jnp.where(column < deep, layer - row + reach, -1)
    stacked = []
    for view in views:
        matrix = jnp.zeros((depth, LANES), F32)
        for t in range(2 * reach + 1):
            matrix = jnp.where(tap == t, depth_taps[view, t], matrix)
        stacked.append(matrix)
    matrix = jnp.concatenate(stacked, axis=0)
    back_high, back_low = split(matrix.T[:padded])
    depth_back[0] = back_high
    depth_back[1] = back_low
    high, low = split(matrix)
    depth_high, depth_low = high[:, :padded], low[:, :padded]

    flip_x, flip_y = is_odd("gx"), is_odd("gy")
    for e in range(rows + 2 * side):
        if e < side:
            extended[e, 0:depth] = jnp.where(flip_x, even_x[e], odd_x[e])
        elif e < side + rows:
            extended[e, 0:depth] = own[:, e - side]
        else:
            extended[e, 0:depth] = jnp.where(flip_x, odd_x[e - side - rows], even_x[e - side - rows])
        even, odd = even_y[e * reach : (e + 1) * reach], odd_y[e * reach : (e + 1) * reach]
        extended[e, depth : depth + reach] = jnp.where(flip_y, even, odd)
        extended[e, depth + reach : deep] = jnp.where(flip_y, odd, even)
        if padded > deep:
            extended[e, deep:padded] = jnp.zeros((padded - deep, lanes), F32)

    for i in range(rows + 2 * side):
        e_high, e_low = split(extended[i])
        blurred[i] = dot(depth_high, e_high) + dot(depth_high, e_low) + dot(depth_low, e_high)

    inward = lax.broadcasted_iota(jnp.int32, (lanes, lanes), 0)
    outward = lax.broadcasted_iota(jnp.int32, (lanes, lanes), 1)
    for turn, view in enumerate(views):
        place = outward
        if turn % 2 == 0:
            place = outward - offsets[view]
            place = jnp.where(place < 0, place + lanes, place)
        tap = (lanes - 1 - place - inward if turn >= 2 else inward - place) + side
        source = row_taps if turn % 2 else column_taps
        matrix = jnp.zeros((lanes, lanes), F32)
        for r in range(width):
            matrix = jnp.where(tap == r, source[view, r], matrix)
        high, low = split(matrix)
        back_high, back_low = split(matrix.T)
        lane_back[turn, 0] = back_high
        lane_back[turn, 1] = back_low
        both = jnp.concatenate([high, high], axis=0)
        factor = row_taps_of(turn, view, row_taps, column_taps, width)
        for i in range(rows):
            layers = pl.ds(turn * depth, depth)
            total = factor[0] * blurred[i, layers]
            for s in range(1, width):
                total = total + factor[s] * blurred[i + s, layers]
            t_high, t_low = split(total)
            predicted[turn, i] = dot(jnp.concatenate([t_high, t_low], axis=1), both) + dot(t_high, low)


def project(turns, row_taps, column_taps, predicted, lane_back, depth_back, kept, mirrored, *rest):
    received = rest[:-7]
    middle, even_pair, odd_pair, arrived, data, backed, spread = rest[-7:]
    _, rows, depth, lanes = predicted.shape
    side = even_pair.shape[0]
    deep = even_pair.shape[1]
    width = 2 * side + 1
    views = [view_of(turns, turn) for turn in range(VIEWS)]
    parts = arrived.shape[0]
    group = LANES // rows
    granule = lax.broadcasted_iota(jnp.int32, (8, LANES), 1) // rows

    me = lax.axis_index("gx")
    for k in range(parts):
        arrived[lax.bitwise_xor(me, k)] = received[k][...]

    for slot in range(2):
        for part in range(0, parts, group):
            for eight in range(0, rows, 8):
                for chunk in range(depth * rows // LANES):
                    held = [
                        arrived[part + s, slot, eight : eight + 8, chunk * LANES : (chunk + 1) * LANES]
                        for s in range(group)
                    ]
                    step = 1
                    while step < group:
                        upper = (granule // step) % 2 == 1
                        swapped = list(held)
                        for s in range(group):
                            if s & step == 0:
                                one, two = held[s], held[s + step]
                                swapped[s] = jnp.where(upper, pltpu.roll(two, step * rows, 1), one)
                                swapped[s + step] = jnp.where(upper, two, pltpu.roll(one, LANES - step * rows, 1))
                        held = swapped
                        step *= 2
                    for s in range(group):
                        data[slot, eight : eight + 8, chunk * group + s, part * rows : part * rows + LANES] = held[s]

    for turn, view in enumerate(views):
        high, low = lane_back[turn, 0], lane_back[turn, 1]
        both = jnp.concatenate([high, high], axis=0)
        for i in range(rows):
            there = rows - 1 - i if turn in (1, 2) else i
            if turn == 0:
                recorded = kept[:, there]
            elif turn == 2:
                recorded = mirrored[:, there]
            else:
                recorded = data[turn // 2, there]
            r_high, r_low = split(recorded / predicted[turn, i])
            backed[turn, i] = dot(jnp.concatenate([r_high, r_low], axis=1), both) + dot(r_high, low)
        factor = row_taps_of(turn, view, row_taps, column_taps, width)
        for e in range(rows + 2 * side):
            total = None
            for i in range(max(0, e - 2 * side), min(rows, e + 1)):
                term = factor[e - i] * backed[turn, i]
                total = term if total is None else total + term
            spread[e, turn * depth : (turn + 1) * depth] = total

    high, low = depth_back[0], depth_back[1]
    both = jnp.concatenate([high, low], axis=1)
    results = []
    for e in range(rows + 2 * side):
        s_high, s_low = split(spread[e])
        result = dot(both, jnp.concatenate([s_high, s_high], axis=0)) + dot(high, s_low)
        result = result[:deep]
        if side <= e < side + rows:
            middle[e - side] = result
        else:
            results.append(result)
    odd = is_odd("gx")
    for i in range(side):
        first, last = results[i], results[side + i]
        even_pair[i] = jnp.where(odd, first, last)
        odd_pair[i] = jnp.where(odd, last, first)


def gather_sides(middle, even_x, odd_x, own, even_pair, odd_pair):
    rows = middle.shape[0]
    side = even_x.shape[0]
    depth = own.shape[1]
    reach = even_pair.shape[0] // rows
    flip_x, flip_y = is_odd("gx"), is_odd("gy")
    for i in range(rows):
        value = middle[i]
        if i < side:
            value = value + jnp.where(flip_x, even_x[i], odd_x[i])
        if i >= rows - side:
            j = i - rows + side
            value = value + jnp.where(flip_x, odd_x[j], even_x[j])
        own[i] = value[:depth]
        before, after = value[depth : depth + reach], value[depth + reach : depth + 2 * reach]
        even_pair[i * reach : (i + 1) * reach] = jnp.where(flip_y, before, after)
        odd_pair[i * reach : (i + 1) * reach] = jnp.where(flip_y, after, before)


def finish(estimate, own, even_y, odd_y, out):
    rows, depth, lanes = own.shape
    reach = even_y.shape[0] // rows
    flip_y = is_odd("gy")
    rest = jnp.zeros((depth - reach, lanes), F32)
    for i in range(rows):
        even, odd = even_y[i * reach : (i + 1) * reach], odd_y[i * reach : (i + 1) * reach]
        first, last = jnp.where(flip_y, even, odd), jnp.where(flip_y, odd, even)
        value = own[i] + jnp.concatenate([first, rest], axis=0) + jnp.concatenate([rest, last], axis=0)
        out[:, i] = estimate[:, i] * value * (1.0 / VIEWS)


def call(body, out_shape, specs, scratch=(), cost=None):
    return pl.pallas_call(
        body,
        out_shape=out_shape,
        in_specs=specs,
        out_specs=jax.tree.map(lambda _: VMEM, out_shape),
        scratch_shapes=scratch,
        compiler_params=PARAMS,
        cost_estimate=cost,
    )


def shards(estimate, recorded, quarter_turns, offsets, depth_taps, row_taps, column_taps):
    depth, rows, lanes = estimate.shape
    reach = (depth_taps.shape[1] - 1) // 2
    side = (row_taps.shape[1] - 1) // 2
    deep = depth + 2 * reach
    padded = -(-deep // 16) * 16
    parts = lax.axis_size("gx")
    even_y, odd_y = pairs(lax.axis_size("gy"))
    even_x, odd_x = pairs(parts)

    first, second = call(edges, (struct(side, depth, lanes),) * 2, [VMEM])(estimate)
    first, second = lax.ppermute(first, "gx", even_x), lax.ppermute(second, "gx", odd_x)
    kept, mirrored, *sent = call(
        prepare,
        (struct(depth, rows, lanes),) * 2 + (struct(2, rows, depth * rows),) * parts,
        [SMEM, SMEM, VMEM],
        [pltpu.VMEM((lanes, depth * rows), F32)],
    )(quarter_turns, offsets, recorded)
    mirrored = lax.ppermute(mirrored, "gx", [(i, parts - 1 - i) for i in range(parts)])
    third, fourth = call(layers_out, (struct((rows + 2 * side) * reach, lanes),) * 2, [VMEM] * 3)(estimate, first, second)
    third, fourth = lax.ppermute(third, "gy", even_y), lax.ppermute(fourth, "gy", odd_y)
    arrived = [sent[0]] + [
        lax.ppermute(sent[k], "gx", [(i, i ^ k) for i in range(parts)]) for k in range(1, parts)
    ]

    predicted, lane_back, depth_back = call(
        predict,
        (
            struct(VIEWS, rows, depth, lanes),
            struct(VIEWS, 2, lanes, lanes, dtype=BF16),
            struct(2, padded, VIEWS * depth, dtype=BF16),
        ),
        [SMEM] * 5 + [VMEM] * 5,
        [
            pltpu.VMEM((rows + 2 * side, padded, lanes), F32),
            pltpu.VMEM((rows + 2 * side, VIEWS * depth, lanes), F32),
        ],
        pl.CostEstimate(flops=4_000_000_000, bytes_accessed=4_000_000, transcendentals=0),
    )(quarter_turns, offsets, depth_taps, row_taps, column_taps, estimate, first, second, third, fourth)

    middle, first, second = call(
        project,
        (struct(rows, deep, lanes), struct(side, deep, lanes), struct(side, deep, lanes)),
        [SMEM] * 3 + [VMEM] * (5 + parts),
        [
            pltpu.VMEM((parts, 2, rows, depth * rows), F32),
            pltpu.VMEM((2, rows, depth, lanes), F32),
            pltpu.VMEM((VIEWS, rows, depth, lanes), F32),
            pltpu.VMEM((rows + 2 * side, VIEWS * depth, lanes), F32),
        ],
        pl.CostEstimate(flops=4_000_000_000, bytes_accessed=4_000_000, transcendentals=0),
    )(quarter_turns, row_taps, column_taps, predicted, lane_back, depth_back, kept, mirrored, *arrived)

    first, second = lax.ppermute(first, "gx", even_x), lax.ppermute(second, "gx", odd_x)
    own, third, fourth = call(
        gather_sides,
        (struct(rows, depth, lanes), struct(rows * reach, lanes), struct(rows * reach, lanes)),
        [VMEM] * 3,
    )(middle, first, second)
    third, fourth = lax.ppermute(third, "gy", even_y), lax.ppermute(fourth, "gy", odd_y)
    return call(finish, struct(depth, rows, lanes), [VMEM] * 4)(estimate, own, third, fourth)


def solution(mesh):
    in_specs = (P("gy", "gx", None), P(None, "gy", "gx", None), P(), P(), P(), P(), P())
    out_specs = P("gy", "gx", None)
    return jax.shard_map(shards, mesh=mesh, in_specs=in_specs, out_specs=out_specs, check_vma=False)
```

```python
import functools

import jax
import jax.numpy as jnp
from jax import lax
from jax.experimental import pallas as pl
from jax.experimental.pallas import tpu as pltpu
from jax.sharding import PartitionSpec as P

VIEWS = 4
LANES = 128
VMEM = pl.BlockSpec(memory_space=pltpu.VMEM)
SMEM = pl.BlockSpec(memory_space=pltpu.SMEM)
PARAMS = pltpu.CompilerParams(vmem_limit_bytes=24 * 1024 * 1024)
F32 = jnp.float32
BF16 = jnp.bfloat16


def struct(*shape, dtype=F32):
    return jax.ShapeDtypeStruct(shape, dtype)


def view_of(turns_ref, turn):
    found = jnp.int32(0)
    for view in range(1, VIEWS):
        found = jnp.where(turns_ref[view] == turn, jnp.int32(view), found)
    return found


def split(value):
    high = value.astype(BF16)
    return high, (value - high.astype(F32)).astype(BF16)


def dot(left, right):
    return jnp.dot(left, right, preferred_element_type=F32)


def pairs(width):
    def swaps(initial):
        return [p for i in range(initial, width - 1, 2) for p in ((i, i + 1), (i + 1, i))]

    return swaps(0), swaps(1)


def is_odd(axis):
    return lax.rem(lax.axis_index(axis), 2) == 1


def pick(turns, recorded, outer):
    rows = recorded.shape[2]
    half = outer.shape[1] // 2
    outer[:, :half] = recorded[0, :, :half]
    outer[:, half:] = recorded[0, :, rows - half :]


def prepare(turns, offsets, recorded, kept, mine, theirs, across):
    depth, rows, lanes = recorded.shape[1:]
    chips, _, _, eight, wide = mine.shape
    side = eight // 2
    me = lax.axis_index("gx")
    kept[...] = recorded[view_of(turns, 0)]
    for slot, turn in enumerate((1, 3)):
        view = view_of(turns, turn)
        volume = recorded[view].reshape(depth * rows, lanes)
        volume = pltpu.roll(volume, lax.rem(lanes - offsets[view], lanes), 1)
        across[...] = volume.T
        for k in range(2 * chips):
            to = lax.bitwise_xor(me, k)
            part = 2 * chips - 1 - to if turn == 1 else to
            block = across[pl.ds(pl.multiple_of(part * rows, rows), rows)]
            outer = jnp.concatenate([block[:side], block[rows - side :]], axis=0)
            for chunk, value in enumerate((outer, block[side : rows - side])):
                if k % 2 == 0:
                    mine[k // 2, chunk, slot] = value
                else:
                    theirs[pl.ds((((k // 2) * 2 + chunk) * 2 + slot) * eight, eight)] = value
    view = view_of(turns, 2)
    fold = wide // lanes
    run = depth // fold
    for q in range(fold):
        inner = recorded[view, q * run : (q + 1) * run, side : rows - side]
        theirs[chips * 4 * eight :, q * lanes : (q + 1) * lanes] = inner.reshape(run * eight, lanes)


def merge(mine, swapped, *outs):
    chips, _, _, eight, _ = mine.shape
    for chunk in range(2):
        for k in range(1, chips):
            out = outs[chunk * (chips - 1) + k - 1]
            for slot in range(2):
                out[slot * eight : (slot + 1) * eight] = mine[k, chunk, slot]
            start = (k * 2 + chunk) * 2 * eight
            out[2 * eight : 4 * eight] = swapped[start : start + 2 * eight]
            if chunk == 1 and k == chips - 1:
                out[4 * eight :] = swapped[chips * 4 * eight :]


def edges(own, even_pair, odd_pair):
    rows = own.shape[1]
    side = even_pair.shape[0]
    odd = is_odd("gx")
    for i in range(side):
        first, last = own[:, i], own[:, rows - side + i]
        even_pair[i] = jnp.where(odd, first, last)
        odd_pair[i] = jnp.where(odd, last, first)


def layers_out(own, from_even, from_odd, even_pair, odd_pair):
    depth, rows, _ = own.shape
    side = from_even.shape[0]
    reach = even_pair.shape[0] // (rows + 2 * side)
    odd_x, odd_y = is_odd("gx"), is_odd("gy")
    for e in range(rows + 2 * side):
        if e < side:
            value = jnp.where(odd_x, from_even[e], from_odd[e])
        elif e < side + rows:
            value = own[:, e - side]
        else:
            value = jnp.where(odd_x, from_odd[e - side - rows], from_even[e - side - rows])
        first, last = value[:reach], value[depth - reach :]
        even_pair[e * reach : (e + 1) * reach] = jnp.where(odd_y, first, last)
        odd_pair[e * reach : (e + 1) * reach] = jnp.where(odd_y, last, first)


def row_taps_of(turn, view, row_taps, column_taps, width):
    source = column_taps if turn % 2 else row_taps
    flipped = turn in (1, 2)
    return [source[view, width - 1 - s if flipped else s] for s in range(width)]


def predict(turns, offsets, depth_taps, row_taps, column_taps, own, even_x, odd_x, even_y, odd_y,
            predicted, lane_back, depth_back, extended, blurred):
    depth, rows, lanes = own.shape
    side = even_x.shape[0]
    reach = even_y.shape[0] // (rows + 2 * side)
    width = 2 * side + 1
    deep = depth + 2 * reach
    padded = extended.shape[1]
    views = [view_of(turns, turn) for turn in range(VIEWS)]

    column = lax.broadcasted_iota(jnp.int32, (depth, LANES), 1)
    row = lax.broadcasted_iota(jnp.int32, (depth, LANES), 0)
    layer = jnp.where(column < depth, column, jnp.where(column < depth + reach, column - depth - reach, column - reach))
    tap = jnp.where(column < deep, layer - row + reach, -1)
    stacked = []
    for view in views:
        matrix = jnp.zeros((depth, LANES), F32)
        for t in range(2 * reach + 1):
            matrix = jnp.where(tap == t, depth_taps[view, t], matrix)
        stacked.append(matrix)
    matrix = jnp.concatenate(stacked, axis=0)
    back_high, back_low = split(matrix.T[:padded])
    depth_back[0] = back_high
    depth_back[1] = back_low
    high, low = split(matrix)
    depth_high, depth_low = high[:, :padded], low[:, :padded]

    flip_x, flip_y = is_odd("gx"), is_odd("gy")
    for e in range(rows + 2 * side):
        if e < side:
            extended[e, 0:depth] = jnp.where(flip_x, even_x[e], odd_x[e])
        elif e < side + rows:
            extended[e, 0:depth] = own[:, e - side]
        else:
            extended[e, 0:depth] = jnp.where(flip_x, odd_x[e - side - rows], even_x[e - side - rows])
        even, odd = even_y[e * reach : (e + 1) * reach], odd_y[e * reach : (e + 1) * reach]
        extended[e, depth : depth + reach] = jnp.where(flip_y, even, odd)
        extended[e, depth + reach : deep] = jnp.where(flip_y, odd, even)
        if padded > deep:
            extended[e, deep:padded] = jnp.zeros((padded - deep, lanes), F32)

    for i in range(rows + 2 * side):
        e_high, e_low = split(extended[i])
        blurred[i] = dot(depth_high, e_high) + dot(depth_high, e_low) + dot(depth_low, e_high)

    inward = lax.broadcasted_iota(jnp.int32, (lanes, lanes), 0)
    outward = lax.broadcasted_iota(jnp.int32, (lanes, lanes), 1)
    for turn, view in enumerate(views):
        place = outward
        if turn % 2 == 0:
            place = outward - offsets[view]
            place = jnp.where(place < 0, place + lanes, place)
        tap = (lanes - 1 - place - inward if turn >= 2 else inward - place) + side
        source = row_taps if turn % 2 else column_taps
        matrix = jnp.zeros((lanes, lanes), F32)
        for r in range(width):
            matrix = jnp.where(tap == r, source[view, r], matrix)
        high, low = split(matrix)
        back_high, back_low = split(matrix.T)
        lane_back[turn, 0] = back_high
        lane_back[turn, 1] = back_low
        both = jnp.concatenate([high, high], axis=0)
        factor = row_taps_of(turn, view, row_taps, column_taps, width)
        for i in range(rows):
            layers = pl.ds(turn * depth, depth)
            total = factor[0] * blurred[i, layers]
            for s in range(1, width):
                total = total + factor[s] * blurred[i + s, layers]
            t_high, t_low = split(total)
            predicted[turn, i] = dot(jnp.concatenate([t_high, t_low], axis=1), both) + dot(t_high, low)


def turned(chunk, mine, swapped, received, arrived, data):
    parts, _, eight, wide = arrived.shape
    depth = data.shape[2]
    rows = wide // depth
    group = LANES // rows
    me = lax.axis_index("gx")
    for k in range(parts // 2):
        for core in range(2):
            source = lax.bitwise_xor(me, 2 * k + core)
            for slot in range(2):
                if k > 0:
                    start = (core * 2 + slot) * eight
                    value = received[k - 1][start : start + eight]
                elif core == 0:
                    value = mine[0, chunk, slot]
                else:
                    start = (chunk * 2 + slot) * eight
                    value = swapped[start : start + eight]
                arrived[source, slot] = value
    granule = lax.broadcasted_iota(jnp.int32, (eight, LANES), 1) // rows
    for slot in range(2):
        for part in range(0, parts, group):
            for piece in range(wide // LANES):
                held = [arrived[part + s, slot, :, piece * LANES : (piece + 1) * LANES] for s in range(group)]
                step = 1
                while step < group:
                    upper = (granule // step) % 2 == 1
                    swapped_now = list(held)
                    for s in range(group):
                        if s & step == 0:
                            one, two = held[s], held[s + step]
                            swapped_now[s] = jnp.where(upper, pltpu.roll(two, step * rows, 1), one)
                            swapped_now[s + step] = jnp.where(upper, two, pltpu.roll(one, LANES - step * rows, 1))
                    held = swapped_now
                    step *= 2
                for s in range(group):
                    data[slot, :, piece * group + s, part * rows : part * rows + LANES] = held[s]


def ratios(row_list, half_turned, predicted, lane_back, kept, data, backed):
    count = len(row_list)
    for turn in range(VIEWS):
        high, low = lane_back[turn, 0], lane_back[turn, 1]
        both = jnp.concatenate([high, high], axis=0)
        for j, i in enumerate(row_list):
            there = count - 1 - j if turn in (1, 2) else j
            if turn == 0:
                recorded = kept[:, i]
            elif turn == 2:
                recorded = half_turned(there)
            else:
                recorded = data[turn // 2, there]
            r_high, r_low = split(recorded / predicted[turn, i])
            backed[turn, j] = dot(jnp.concatenate([r_high, r_low], axis=1), both) + dot(r_high, low)


def spread_row(e, turn, factor, row_list, side, backed):
    total = None
    for j, i in enumerate(row_list):
        if 0 <= e - i <= 2 * side:
            term = factor[e - i] * backed[turn, j]
            total = term if total is None else total + term
    return total


def depth_blur(high, both, value):
    s_high, s_low = split(value)
    return dot(both, jnp.concatenate([s_high, s_high], axis=0)) + dot(high, s_low)


def project_outer(turns, row_taps, column_taps, predicted, lane_back, depth_back, kept, mirrored, mine, swapped, *rest):
    received, (even_pair, odd_pair, partial, arrived, data, backed) = rest[:-6], rest[-6:]
    _, rows, depth, lanes = predicted.shape
    side, deep, _ = even_pair.shape
    row_list = [*range(side), *range(rows - side, rows)]
    turned(0, mine, swapped, received, arrived, data)
    ratios(row_list, lambda j: mirrored[:, j], predicted, lane_back, kept, data, backed)
    factors = [
        row_taps_of(turn, view_of(turns, turn), row_taps, column_taps, 2 * side + 1) for turn in range(VIEWS)
    ]
    high, low = depth_back[0], depth_back[1]
    both = jnp.concatenate([high, low], axis=1)
    results = []
    for e in [*range(side), *range(rows + side, rows + 2 * side)]:
        value = jnp.concatenate(
            [spread_row(e, turn, factors[turn], row_list, side, backed) for turn in range(VIEWS)], axis=0
        )
        results.append(depth_blur(high, both, value)[:deep])
    odd = is_odd("gx")
    for i in range(side):
        first, last = results[i], results[side + i]
        even_pair[i] = jnp.where(odd, first, last)
        odd_pair[i] = jnp.where(odd, last, first)
    for e in range(side, rows + side):
        for turn in range(VIEWS):
            total = spread_row(e, turn, factors[turn], row_list, side, backed)
            partial[e - side, turn * depth : (turn + 1) * depth] = total


def project_inner(turns, row_taps, column_taps, predicted, lane_back, depth_back, kept, partial, mine, swapped, *rest):
    received, (middle, arrived, data, backed, inner) = rest[:-5], rest[-5:]
    _, rows, depth, lanes = predicted.shape
    deep = middle.shape[1]
    _, _, eight, wide = arrived.shape
    side = (rows - eight) // 2
    row_list = [*range(side, rows - side)]
    fold = wide // lanes
    run = depth // fold

    for q in range(fold):
        block = received[-1][4 * eight :, q * lanes : (q + 1) * lanes]
        inner[q * run : (q + 1) * run] = block.reshape(run, eight, lanes)

    turned(1, mine, swapped, received, arrived, data)
    ratios(row_list, lambda j: inner[:, j], predicted, lane_back, kept, data, backed)
    factors = [
        row_taps_of(turn, view_of(turns, turn), row_taps, column_taps, 2 * side + 1) for turn in range(VIEWS)
    ]
    high, low = depth_back[0], depth_back[1]
    both = jnp.concatenate([high, low], axis=1)
    for e in range(side, rows + side):
        value = partial[e - side] + jnp.concatenate(
            [spread_row(e, turn, factors[turn], row_list, side, backed) for turn in range(VIEWS)], axis=0
        )
        middle[e - side] = depth_blur(high, both, value)[:deep]


def gather_sides(middle, even_x, odd_x, own, even_pair, odd_pair):
    rows = middle.shape[0]
    side = even_x.shape[0]
    depth = own.shape[1]
    reach = even_pair.shape[0] // rows
    flip_x, flip_y = is_odd("gx"), is_odd("gy")
    for i in range(rows):
        value = middle[i]
        if i < side:
            value = value + jnp.where(flip_x, even_x[i], odd_x[i])
        if i >= rows - side:
            j = i - rows + side
            value = value + jnp.where(flip_x, odd_x[j], even_x[j])
        own[i] = value[:depth]
        before, after = value[depth : depth + reach], value[depth + reach : depth + 2 * reach]
        even_pair[i * reach : (i + 1) * reach] = jnp.where(flip_y, before, after)
        odd_pair[i * reach : (i + 1) * reach] = jnp.where(flip_y, after, before)


def finish(estimate, own, even_y, odd_y, out):
    rows, depth, lanes = own.shape
    reach = even_y.shape[0] // rows
    flip_y = is_odd("gy")
    rest = jnp.zeros((depth - reach, lanes), F32)
    for i in range(rows):
        even, odd = even_y[i * reach : (i + 1) * reach], odd_y[i * reach : (i + 1) * reach]
        first, last = jnp.where(flip_y, even, odd), jnp.where(flip_y, odd, even)
        value = own[i] + jnp.concatenate([first, rest], axis=0) + jnp.concatenate([rest, last], axis=0)
        out[:, i] = estimate[:, i] * value * (1.0 / VIEWS)


def call(body, out_shape, specs, scratch=(), cost=None):
    return pl.pallas_call(
        body,
        out_shape=out_shape,
        in_specs=specs,
        out_specs=jax.tree.map(lambda _: VMEM, out_shape),
        scratch_shapes=scratch,
        compiler_params=PARAMS,
        cost_estimate=cost,
    )


def shards(estimate, recorded, quarter_turns, offsets, depth_taps, row_taps, column_taps):
    depth, rows, lanes = estimate.shape
    reach = (depth_taps.shape[1] - 1) // 2
    side = (row_taps.shape[1] - 1) // 2
    deep = depth + 2 * reach
    padded = -(-deep // 16) * 16
    parts = lax.axis_size("gx")
    even_y, odd_y = pairs(lax.axis_size("gy"))
    even_x, odd_x = pairs(parts)

    first, second = call(edges, (struct(side, depth, lanes),) * 2, [VMEM])(estimate)
    first, second = lax.ppermute(first, "gx", even_x), lax.ppermute(second, "gx", odd_x)
    mirror = [(i, parts - 1 - i) for i in range(parts)]
    outer = pl.pallas_call(
        pick,
        out_shape=struct(depth, 2 * side, lanes),
        grid_spec=pltpu.PrefetchScalarGridSpec(
            num_scalar_prefetch=1,
            grid=(1,),
            in_specs=[pl.BlockSpec((1, depth, rows, lanes), lambda i, turns: (view_of(turns, 2), 0, 0, 0))],
            out_specs=pl.BlockSpec((depth, 2 * side, lanes), lambda i, turns: (0, 0, 0)),
        ),
        compiler_params=PARAMS,
    )(quarter_turns, recorded)
    outer = lax.ppermute(outer, "gx", mirror)
    eight, wide, chips = rows // 2, depth * rows, parts // 2
    extra = depth * eight * lanes // wide
    kept, mine, theirs = call(
        prepare,
        (struct(depth, rows, lanes), struct(chips, 2, 2, eight, wide), struct(chips * 4 * eight + extra, wide)),
        [SMEM, SMEM, VMEM],
        [pltpu.VMEM((lanes, depth * rows), F32)],
    )(quarter_turns, offsets, recorded)
    swapped = lax.ppermute(theirs, "gx", [(i, i ^ 1) for i in range(parts)])
    messages = call(
        merge,
        (struct(4 * eight, wide),) * (2 * chips - 3) + (struct(4 * eight + extra, wide),),
        [VMEM] * 2,
    )(mine, swapped)
    third, fourth = call(layers_out, (struct((rows + 2 * side) * reach, lanes),) * 2, [VMEM] * 3)(estimate, first, second)
    third, fourth = lax.ppermute(third, "gy", even_y), lax.ppermute(fourth, "gy", odd_y)
    order = [*range(chips - 1, 0, -1)]
    moved = {
        (chunk, k): lax.ppermute(
            messages[chunk * (chips - 1) + k - 1], "gx", [(i, i ^ (2 * k)) for i in range(parts)]
        )
        for chunk in range(2)
        for k in order
    }

    predicted, lane_back, depth_back = call(
        predict,
        (
            struct(VIEWS, rows, depth, lanes),
            struct(VIEWS, 2, lanes, lanes, dtype=BF16),
            struct(2, padded, VIEWS * depth, dtype=BF16),
        ),
        [SMEM] * 5 + [VMEM] * 5,
        [
            pltpu.VMEM((rows + 2 * side, padded, lanes), F32),
            pltpu.VMEM((rows + 2 * side, VIEWS * depth, lanes), F32),
        ],
        pl.CostEstimate(flops=4_000_000_000, bytes_accessed=4_000_000, transcendentals=0),
    )(quarter_turns, offsets, depth_taps, row_taps, column_taps, estimate, first, second, third, fourth)

    scratch = [
        pltpu.VMEM((parts, 2, eight, wide), F32),
        pltpu.VMEM((2, eight, depth, lanes), F32),
        pltpu.VMEM((VIEWS, eight, depth, lanes), F32),
    ]
    first, second, partial = call(
        project_outer,
        (struct(side, deep, lanes),) * 2 + (struct(rows, VIEWS * depth, lanes),),
        [SMEM] * 3 + [VMEM] * (6 + chips),
        scratch,
        pl.CostEstimate(flops=2_000_000_000, bytes_accessed=4_000_000, transcendentals=0),
    )(quarter_turns, row_taps, column_taps, predicted, lane_back, depth_back, kept, outer, mine, swapped,
      *[moved[0, k] for k in range(1, chips)])
    first, second = lax.ppermute(first, "gx", even_x), lax.ppermute(second, "gx", odd_x)
    middle = call(
        project_inner,
        struct(rows, deep, lanes),
        [SMEM] * 3 + [VMEM] * (6 + chips),
        [*scratch, pltpu.VMEM((depth, eight, lanes), F32)],
        pl.CostEstimate(flops=2_000_000_000, bytes_accessed=4_000_000, transcendentals=0),
    )(quarter_turns, row_taps, column_taps, predicted, lane_back, depth_back, kept, partial, mine, swapped,
      *[moved[1, k] for k in range(1, chips)])
    own, third, fourth = call(
        gather_sides,
        (struct(rows, depth, lanes), struct(rows * reach, lanes), struct(rows * reach, lanes)),
        [VMEM] * 3,
    )(middle, first, second)
    third, fourth = lax.ppermute(third, "gy", even_y), lax.ppermute(fourth, "gy", odd_y)
    return call(finish, struct(depth, rows, lanes), [VMEM] * 4)(estimate, own, third, fourth)


def solution(mesh):
    in_specs = (P("gy", "gx", None), P(None, "gy", "gx", None), P(), P(), P(), P(), P())
    out_specs = P("gy", "gx", None)
    return jax.shard_map(shards, mesh=mesh, in_specs=in_specs, out_specs=out_specs, check_vma=False)
```

```python
import functools

import jax
import jax.numpy as jnp
from jax import lax
from jax.experimental import pallas as pl
from jax.experimental.pallas import tpu as pltpu
from jax.sharding import PartitionSpec as P

VIEWS = 4
LANES = 128
VMEM = pl.BlockSpec(memory_space=pltpu.VMEM)
ORDER = pl.BlockSpec(memory_space=pl.ANY)
SMEM = pl.BlockSpec(memory_space=pltpu.SMEM)
PARAMS = pltpu.CompilerParams(vmem_limit_bytes=24 * 1024 * 1024)
F32 = jnp.float32
BF16 = jnp.bfloat16
COST = pl.CostEstimate(flops=1, bytes_accessed=1, transcendentals=0)


def struct(*shape, dtype=F32):
    return jax.ShapeDtypeStruct(shape, dtype)


def view_of(turns_ref, turn):
    found = jnp.int32(0)
    for view in range(1, VIEWS):
        found = jnp.where(turns_ref[view] == turn, jnp.int32(view), found)
    return found


def split(value):
    high = value.astype(BF16)
    return high, (value - high.astype(F32)).astype(BF16)


def dot(left, right):
    return jnp.dot(left, right, preferred_element_type=F32)


def pairs(width):
    def swaps(initial):
        return [p for i in range(initial, width - 1, 2) for p in ((i, i + 1), (i + 1, i))]

    return swaps(0), swaps(1)


def is_odd(axis):
    return lax.rem(lax.axis_index(axis), 2) == 1


def pick(turns, recorded, later, outer, inner):
    rows = recorded.shape[2]
    half = outer.shape[1] // 2
    outer[:, :half] = recorded[0, :, :half]
    outer[:, half:] = recorded[0, :, rows - half :]
    inner[...] = recorded[0, :, half : rows - half]


def prepare(turns, offsets, recorded, later, kept, mine, theirs, across):
    depth, rows, lanes = recorded.shape[1:]
    chips, _, _, wide = mine.shape
    me = lax.axis_index("gx")
    kept[...] = recorded[view_of(turns, 0)]
    for slot, turn in enumerate((1, 3)):
        view = view_of(turns, turn)
        volume = recorded[view].reshape(depth * rows, lanes)
        volume = pltpu.roll(volume, lax.rem(lanes - offsets[view], lanes), 1)
        across[...] = volume.T
        for k in range(2 * chips):
            to = lax.bitwise_xor(me, k)
            part = 2 * chips - 1 - to if turn == 1 else to
            block = across[pl.ds(pl.multiple_of(part * rows, rows), rows)]
            if k % 2 == 0:
                mine[k // 2, slot] = block
            else:
                theirs[k // 2, slot] = block


def merge(mine, swapped, inner, inner_out, *outs):
    depth, count, lanes = inner.shape
    inner_out[: depth * count] = inner[...].reshape(depth * count, lanes)
    inner_out[depth * count :] = jnp.zeros((inner_out.shape[0] - depth * count, lanes), F32)
    for k in range(1, mine.shape[0]):
        for slot in range(2):
            outs[k - 1][0, slot] = mine[k, slot]
            outs[k - 1][1, slot] = swapped[k, slot]


def ends(own, even_pair, odd_pair):
    reach = even_pair.shape[0]
    first, last = own[:reach], own[own.shape[0] - reach :]
    odd = is_odd("gy")
    even_pair[...] = jnp.where(odd, first, last)
    odd_pair[...] = jnp.where(odd, last, first)


def edges(own, even_y, odd_y, later, later_too, even_pair, odd_pair):
    depth, rows, _ = own.shape
    reach = even_y.shape[0]
    side = even_pair.shape[0]
    flip_x, flip_y = is_odd("gx"), is_odd("gy")
    for i in range(side):
        first, last = i, rows - side + i
        for start, upper, lower in (
            (0, own[:, first], own[:, last]),
            (depth, jnp.where(flip_y, even_y[:, first], odd_y[:, first]), jnp.where(flip_y, even_y[:, last], odd_y[:, last])),
            (depth + reach, jnp.where(flip_y, odd_y[:, first], even_y[:, first]), jnp.where(flip_y, odd_y[:, last], even_y[:, last])),
        ):
            stop = start + upper.shape[0]
            even_pair[i, start:stop] = jnp.where(flip_x, upper, lower)
            odd_pair[i, start:stop] = jnp.where(flip_x, lower, upper)


def row_taps_of(turn, view, row_taps, column_taps, width):
    source = column_taps if turn % 2 else row_taps
    flipped = turn in (1, 2)
    return [source[view, width - 1 - s if flipped else s] for s in range(width)]


def predict(turns, offsets, depth_taps, row_taps, column_taps, own, even_x, odd_x, even_y, odd_y,
            predicted, lane_back, depth_back, half_back, extended, blurred):
    depth, rows, lanes = own.shape
    side = even_x.shape[0]
    reach = even_y.shape[0]
    width = 2 * side + 1
    deep = depth + 2 * reach
    padded = extended.shape[1]
    views = [view_of(turns, turn) for turn in range(VIEWS)]

    column = lax.broadcasted_iota(jnp.int32, (depth, LANES), 1)
    row = lax.broadcasted_iota(jnp.int32, (depth, LANES), 0)
    layer = jnp.where(column < depth, column, jnp.where(column < depth + reach, column - depth - reach, column - reach))
    tap = jnp.where(column < deep, layer - row + reach, -1)
    stacked = []
    for view in views:
        matrix = jnp.zeros((depth, LANES), F32)
        for t in range(2 * reach + 1):
            matrix = jnp.where(tap == t, depth_taps[view, t], matrix)
        stacked.append(matrix)
    matrix = jnp.concatenate(stacked, axis=0)
    back_high, back_low = split(matrix.T[:padded])
    depth_back[0] = back_high
    depth_back[1] = back_low
    half = slice(2 * depth, 3 * depth)
    half_back[...] = jnp.concatenate([back_high[:, half], back_low[:, half], back_high[:, half]], axis=1)
    high, low = split(matrix)
    depth_high, depth_low = high[:, :padded], low[:, :padded]

    flip_x, flip_y = is_odd("gx"), is_odd("gy")
    for e in range(rows + 2 * side):
        if side <= e < side + rows:
            i = e - side
            even, odd = even_y[:, i], odd_y[:, i]
            extended[e, 0:depth] = own[:, i]
            extended[e, depth : depth + reach] = jnp.where(flip_y, even, odd)
            extended[e, depth + reach : deep] = jnp.where(flip_y, odd, even)
        elif e < side:
            extended[e, 0:deep] = jnp.where(flip_x, even_x[e], odd_x[e])
        else:
            i = e - side - rows
            extended[e, 0:deep] = jnp.where(flip_x, odd_x[i], even_x[i])
        if padded > deep:
            extended[e, deep:padded] = jnp.zeros((padded - deep, lanes), F32)

    for i in range(rows + 2 * side):
        e_high, e_low = split(extended[i])
        blurred[i] = dot(depth_high, e_high) + dot(depth_high, e_low) + dot(depth_low, e_high)

    inward = lax.broadcasted_iota(jnp.int32, (lanes, lanes), 0)
    outward = lax.broadcasted_iota(jnp.int32, (lanes, lanes), 1)
    for turn, view in enumerate(views):
        place = outward
        if turn % 2 == 0:
            place = outward - offsets[view]
            place = jnp.where(place < 0, place + lanes, place)
        tap = (lanes - 1 - place - inward if turn >= 2 else inward - place) + side
        source = row_taps if turn % 2 else column_taps
        matrix = jnp.zeros((lanes, lanes), F32)
        for r in range(width):
            matrix = jnp.where(tap == r, source[view, r], matrix)
        high, low = split(matrix)
        back_high, back_low = split(matrix.T)
        lane_back[turn, 0] = back_high
        lane_back[turn, 1] = back_low
        both = jnp.concatenate([high, high], axis=0)
        factor = row_taps_of(turn, view, row_taps, column_taps, width)
        for i in range(rows):
            layers = pl.ds(turn * depth, depth)
            total = factor[0] * blurred[i, layers]
            for s in range(1, width):
                total = total + factor[s] * blurred[i + s, layers]
            t_high, t_low = split(total)
            predicted[turn, i] = dot(jnp.concatenate([t_high, t_low], axis=1), both) + dot(t_high, low)


def turned(mine, swapped, received, arrived, data):
    parts, _, rows, wide = arrived.shape
    group = LANES // rows
    me = lax.axis_index("gx")
    for k in range(parts // 2):
        for core in range(2):
            source = lax.bitwise_xor(me, 2 * k + core)
            if k > 0:
                arrived[source] = received[k - 1][core]
            else:
                arrived[source] = swapped[0] if core else mine[0]
    granule = lax.broadcasted_iota(jnp.int32, (8, LANES), 1) // rows
    for slot in range(2):
        for part in range(0, parts, group):
            for eight in range(0, rows, 8):
                for piece in range(wide // LANES):
                    held = [
                        arrived[part + s, slot, eight : eight + 8, piece * LANES : (piece + 1) * LANES]
                        for s in range(group)
                    ]
                    step = 1
                    while step < group:
                        upper = (granule // step) % 2 == 1
                        crossed = list(held)
                        for s in range(group):
                            if s & step == 0:
                                one, two = held[s], held[s + step]
                                crossed[s] = jnp.where(upper, pltpu.roll(two, step * rows, 1), one)
                                crossed[s + step] = jnp.where(upper, two, pltpu.roll(one, LANES - step * rows, 1))
                        held = crossed
                        step *= 2
                    for s in range(group):
                        data[slot, eight : eight + 8, piece * group + s, part * rows : part * rows + LANES] = held[s]


def lane_blur(recorded, predicted, back):
    high, low = back[0], back[1]
    r_high, r_low = split(recorded / predicted)
    both = jnp.concatenate([high, high], axis=0)
    return dot(jnp.concatenate([r_high, r_low], axis=1), both) + dot(r_high, low)


def spread_row(e, factor, row_list, backed):
    total = None
    for i in row_list:
        if 0 <= e - i < len(factor):
            term = factor[e - i] * backed[i]
            total = term if total is None else total + term
    return jnp.zeros(backed.shape[1:], F32) if total is None else total


def project(turns, row_taps, column_taps, predicted, lane_back, depth_back, kept, outer, mine, swapped, *rest):
    received, (middle, even_pair, odd_pair, arrived, data, backed) = rest[:-6], rest[-6:]
    _, rows, depth, lanes = predicted.shape
    side, deep, _ = even_pair.shape
    turned(mine, swapped, received, arrived, data)
    row_lists = [range(rows)] * VIEWS
    row_lists[2] = [*range(side), *range(rows - side, rows)]
    for turn in range(VIEWS):
        for j, i in enumerate(row_lists[turn]):
            if turn == 0:
                recorded = kept[:, i]
            elif turn == 2:
                recorded = outer[:, 2 * side - 1 - j]
            else:
                recorded = data[turn // 2, rows - 1 - i if turn == 1 else i]
            backed[turn, i] = lane_blur(recorded, predicted[turn, i], lane_back.at[turn])
    factors = [
        row_taps_of(turn, view_of(turns, turn), row_taps, column_taps, 2 * side + 1) for turn in range(VIEWS)
    ]
    high, low = depth_back[0], depth_back[1]
    both = jnp.concatenate([high, low], axis=1)
    results = []
    for e in range(rows + 2 * side):
        value = jnp.concatenate(
            [spread_row(e, factors[turn], row_lists[turn], backed.at[turn]) for turn in range(VIEWS)], axis=0
        )
        s_high, s_low = split(value)
        result = dot(both, jnp.concatenate([s_high, s_high], axis=0)) + dot(high, s_low)
        if side <= e < side + rows:
            middle[e - side] = result[:deep]
        else:
            results.append(result[:deep])
    odd = is_odd("gx")
    for i in range(side):
        first, last = results[i], results[side + i]
        even_pair[i] = jnp.where(odd, first, last)
        odd_pair[i] = jnp.where(odd, last, first)


def project_half(turns, row_taps, column_taps, predicted, lane_back, half_back, flat, partial, middle, backed, inner):
    _, rows, depth, lanes = predicted.shape
    deep = middle.shape[1]
    side = (rows - inner.shape[1]) // 2
    inner[...] = flat[: depth * inner.shape[1]].reshape(inner.shape)
    row_list = range(side, rows - side)
    for i in row_list:
        backed[i] = lane_blur(inner[:, rows - side - 1 - i], predicted[2, i], lane_back.at[2])
    factor = row_taps_of(2, view_of(turns, 2), row_taps, column_taps, 2 * side + 1)
    back = half_back[...]
    for e in range(rows):
        s_high, s_low = split(spread_row(e + side, factor, row_list, backed))
        result = dot(back, jnp.concatenate([s_high, s_high, s_low], axis=0))
        middle[e] = partial[e] + result[:deep]


def gather_sides(middle, even_x, odd_x, own, even_pair, odd_pair):
    rows = middle.shape[0]
    side = even_x.shape[0]
    depth = own.shape[1]
    reach = even_pair.shape[0] // rows
    flip_x, flip_y = is_odd("gx"), is_odd("gy")
    for i in range(rows):
        value = middle[i]
        if i < side:
            value = value + jnp.where(flip_x, even_x[i], odd_x[i])
        if i >= rows - side:
            j = i - rows + side
            value = value + jnp.where(flip_x, odd_x[j], even_x[j])
        own[i] = value[:depth]
        before, after = value[depth : depth + reach], value[depth + reach : depth + 2 * reach]
        even_pair[i * reach : (i + 1) * reach] = jnp.where(flip_y, before, after)
        odd_pair[i * reach : (i + 1) * reach] = jnp.where(flip_y, after, before)


def finish(estimate, own, even_y, odd_y, out):
    rows, depth, lanes = own.shape
    reach = even_y.shape[0] // rows
    flip_y = is_odd("gy")
    rest = jnp.zeros((depth - reach, lanes), F32)
    for i in range(rows):
        even, odd = even_y[i * reach : (i + 1) * reach], odd_y[i * reach : (i + 1) * reach]
        first, last = jnp.where(flip_y, even, odd), jnp.where(flip_y, odd, even)
        value = own[i] + jnp.concatenate([first, rest], axis=0) + jnp.concatenate([rest, last], axis=0)
        out[:, i] = estimate[:, i] * value * (1.0 / VIEWS)


def call(body, out_shape, specs, scratch=()):
    return pl.pallas_call(
        body,
        out_shape=out_shape,
        in_specs=specs,
        out_specs=jax.tree.map(lambda _: VMEM, out_shape),
        scratch_shapes=scratch,
        compiler_params=PARAMS,
        cost_estimate=COST,
    )


def shards(estimate, recorded, quarter_turns, offsets, depth_taps, row_taps, column_taps):
    depth, rows, lanes = estimate.shape
    reach = (depth_taps.shape[1] - 1) // 2
    side = (row_taps.shape[1] - 1) // 2
    deep = depth + 2 * reach
    padded = -(-deep // 16) * 16
    parts = lax.axis_size("gx")
    even_y, odd_y = pairs(lax.axis_size("gy"))
    even_x, odd_x = pairs(parts)

    third, fourth = call(ends, (struct(reach, rows, lanes),) * 2, [VMEM])(estimate)
    outer, inner = pl.pallas_call(
        pick,
        out_shape=(struct(depth, 2 * side, lanes), struct(depth, rows - 2 * side, lanes)),
        grid_spec=pltpu.PrefetchScalarGridSpec(
            num_scalar_prefetch=1,
            grid=(1,),
            in_specs=[
                pl.BlockSpec((1, depth, rows, lanes), lambda i, turns: (view_of(turns, 2), 0, 0, 0)),
                ORDER,
            ],
            out_specs=[
                pl.BlockSpec((depth, 2 * side, lanes), lambda i, turns: (0, 0, 0)),
                pl.BlockSpec((depth, rows - 2 * side, lanes), lambda i, turns: (0, 0, 0)),
            ],
        ),
        compiler_params=PARAMS,
        cost_estimate=COST,
    )(quarter_turns, recorded, third)
    wide, chips = depth * rows, parts // 2
    kept, mine, theirs = call(
        prepare,
        (struct(depth, rows, lanes),) + (struct(chips, 2, rows, wide),) * 2,
        [SMEM, SMEM, VMEM, ORDER],
        [pltpu.VMEM((lanes, wide), F32)],
    )(quarter_turns, offsets, recorded, outer)
    third, fourth = lax.ppermute(third, "gy", even_y), lax.ppermute(fourth, "gy", odd_y)
    mirror = [(i, parts - 1 - i) for i in range(parts)]
    outer = lax.ppermute(outer, "gx", mirror)
    swapped = lax.ppermute(theirs, "gx", [(i, i ^ 1) for i in range(parts)])
    inner, *messages = call(
        merge,
        (struct(side * deep + 8, lanes),) + (struct(2, 2, rows, wide),) * (chips - 1),
        [VMEM] * 3,
    )(mine, swapped, inner)
    moved = {
        k: lax.ppermute(messages[k - 1], "gx", [(i, i ^ (2 * k)) for i in range(parts)])
        for k in range(chips - 1, 0, -1)
    }
    inner = lax.ppermute(inner, "gx", mirror)
    first, second = call(edges, (struct(side, deep, lanes),) * 2, [VMEM] * 3 + [ORDER] * 2)(
        estimate, third, fourth, outer, messages[0]
    )
    first, second = lax.ppermute(first, "gx", even_x), lax.ppermute(second, "gx", odd_x)

    predicted, lane_back, depth_back, half_back = call(
        predict,
        (
            struct(VIEWS, rows, depth, lanes),
            struct(VIEWS, 2, lanes, lanes, dtype=BF16),
            struct(2, padded, VIEWS * depth, dtype=BF16),
            struct(padded, 3 * depth, dtype=BF16),
        ),
        [SMEM] * 5 + [VMEM] * 5,
        [
            pltpu.VMEM((rows + 2 * side, padded, lanes), F32),
            pltpu.VMEM((rows + 2 * side, VIEWS * depth, lanes), F32),
        ],
    )(quarter_turns, offsets, depth_taps, row_taps, column_taps, estimate, first, second, third, fourth)

    middle, first, second = call(
        project,
        (struct(rows, deep, lanes), struct(side, deep, lanes), struct(side, deep, lanes)),
        [SMEM] * 3 + [VMEM] * (6 + chips),
        [
            pltpu.VMEM((parts, 2, rows, wide), F32),
            pltpu.VMEM((2, rows, depth, lanes), F32),
            pltpu.VMEM((VIEWS, rows, depth, lanes), F32),
        ],
    )(quarter_turns, row_taps, column_taps, predicted, lane_back, depth_back, kept, outer, mine, swapped,
      *[moved[k] for k in range(1, chips)])
    first, second = lax.ppermute(first, "gx", even_x), lax.ppermute(second, "gx", odd_x)
    middle = call(
        project_half,
        struct(rows, deep, lanes),
        [SMEM] * 3 + [VMEM] * 5,
        [pltpu.VMEM((rows, depth, lanes), F32), pltpu.VMEM((depth, rows - 2 * side, lanes), F32)],
    )(quarter_turns, row_taps, column_taps, predicted, lane_back, half_back, inner, middle)
    own, third, fourth = call(
        gather_sides,
        (struct(rows, depth, lanes), struct(rows * reach, lanes), struct(rows * reach, lanes)),
        [VMEM] * 3,
    )(middle, first, second)
    third, fourth = lax.ppermute(third, "gy", even_y), lax.ppermute(fourth, "gy", odd_y)
    return call(finish, struct(depth, rows, lanes), [VMEM] * 4)(estimate, own, third, fourth)


def solution(mesh):
    in_specs = (P("gy", "gx", None), P(None, "gy", "gx", None), P(), P(), P(), P(), P())
    out_specs = P("gy", "gx", None)
    return jax.shard_map(shards, mesh=mesh, in_specs=in_specs, out_specs=out_specs, check_vma=False)
```

```python
import functools

import jax
import jax.numpy as jnp
from jax import lax
from jax.experimental import pallas as pl
from jax.experimental.pallas import tpu as pltpu
from jax.sharding import PartitionSpec as P

VIEWS = 4
LANES = 128
VMEM = pl.BlockSpec(memory_space=pltpu.VMEM)
ORDER = pl.BlockSpec(memory_space=pl.ANY)
SMEM = pl.BlockSpec(memory_space=pltpu.SMEM)
PARAMS = pltpu.CompilerParams(vmem_limit_bytes=24 * 1024 * 1024)
F32 = jnp.float32
BF16 = jnp.bfloat16
COST = pl.CostEstimate(flops=1, bytes_accessed=1, transcendentals=0)


def struct(*shape, dtype=F32):
    return jax.ShapeDtypeStruct(shape, dtype)


def view_of(turns_ref, turn):
    found = jnp.int32(0)
    for view in range(1, VIEWS):
        found = jnp.where(turns_ref[view] == turn, jnp.int32(view), found)
    return found


def split(value):
    high = value.astype(BF16)
    return high, (value - high.astype(F32)).astype(BF16)


def dot(left, right):
    return jnp.dot(left, right, preferred_element_type=F32)


def pairs(width):
    def swaps(initial):
        return [p for i in range(initial, width - 1, 2) for p in ((i, i + 1), (i + 1, i))]

    return swaps(0), swaps(1)


def is_odd(axis):
    return lax.rem(lax.axis_index(axis), 2) == 1


def pick(turns, recorded, later, outer, inner):
    rows = recorded.shape[2]
    half = outer.shape[1] // 2
    outer[:, :half] = recorded[0, :, :half]
    outer[:, half:] = recorded[0, :, rows - half :]
    inner[...] = recorded[0, :, half : rows - half]


def prepare(turns, offsets, recorded, later, kept, mine, theirs, across):
    depth, rows, lanes = recorded.shape[1:]
    chips, _, _, wide = mine.shape
    me = lax.axis_index("gx")
    kept[...] = recorded[view_of(turns, 0)]
    for slot, turn in enumerate((1, 3)):
        view = view_of(turns, turn)
        volume = recorded[view].reshape(depth * rows, lanes)
        volume = pltpu.roll(volume, lax.rem(lanes - offsets[view], lanes), 1)
        across[...] = volume.T
        for k in range(2 * chips):
            to = lax.bitwise_xor(me, k)
            part = 2 * chips - 1 - to if turn == 1 else to
            block = across[pl.ds(pl.multiple_of(part * rows, rows), rows)]
            if k % 2 == 0:
                mine[k // 2, slot] = block
            else:
                theirs[k // 2, slot] = block


def merge(mine, swapped, *outs):
    for k in range(1, mine.shape[0]):
        for slot in range(2):
            outs[k - 1][0, slot] = mine[k, slot]
            outs[k - 1][1, slot] = swapped[k, slot]


def hold(inner, *rest):
    flat = rest[-1]
    depth, count, lanes = inner.shape
    flat[: depth * count] = inner[...].reshape(depth * count, lanes)
    flat[depth * count :] = jnp.zeros((flat.shape[0] - depth * count, lanes), F32)


def edges(own, even_pair, odd_pair):
    rows = own.shape[1]
    side = even_pair.shape[0]
    odd = is_odd("gx")
    for i in range(side):
        first, last = own[:, i], own[:, rows - side + i]
        even_pair[i] = jnp.where(odd, first, last)
        odd_pair[i] = jnp.where(odd, last, first)


def layers_out(own, from_even, from_odd, even_pair, odd_pair):
    depth, rows, _ = own.shape
    side = from_even.shape[0]
    reach = even_pair.shape[0] // (rows + 2 * side)
    odd_x, odd_y = is_odd("gx"), is_odd("gy")
    for e in range(rows + 2 * side):
        if e < side:
            value = jnp.where(odd_x, from_even[e], from_odd[e])
        elif e < side + rows:
            value = own[:, e - side]
        else:
            value = jnp.where(odd_x, from_odd[e - side - rows], from_even[e - side - rows])
        first, last = value[:reach], value[depth - reach :]
        even_pair[e * reach : (e + 1) * reach] = jnp.where(odd_y, first, last)
        odd_pair[e * reach : (e + 1) * reach] = jnp.where(odd_y, last, first)


def row_taps_of(turn, view, row_taps, column_taps, width):
    source = column_taps if turn % 2 else row_taps
    flipped = turn in (1, 2)
    return [source[view, width - 1 - s if flipped else s] for s in range(width)]


def predict(turns, offsets, depth_taps, row_taps, column_taps, own, even_x, odd_x, even_y, odd_y,
            predicted, lane_back, depth_back, half_back, extended, blurred):
    depth, rows, lanes = own.shape
    side = even_x.shape[0]
    reach = even_y.shape[0] // (rows + 2 * side)
    width = 2 * side + 1
    deep = depth + 2 * reach
    padded = extended.shape[1]
    views = [view_of(turns, turn) for turn in range(VIEWS)]

    column = lax.broadcasted_iota(jnp.int32, (depth, LANES), 1)
    row = lax.broadcasted_iota(jnp.int32, (depth, LANES), 0)
    layer = jnp.where(column < depth, column, jnp.where(column < depth + reach, column - depth - reach, column - reach))
    tap = jnp.where(column < deep, layer - row + reach, -1)
    stacked = []
    for view in views:
        matrix = jnp.zeros((depth, LANES), F32)
        for t in range(2 * reach + 1):
            matrix = jnp.where(tap == t, depth_taps[view, t], matrix)
        stacked.append(matrix)
    matrix = jnp.concatenate(stacked, axis=0)
    back_high, back_low = split(matrix.T[:padded])
    depth_back[0] = back_high
    depth_back[1] = back_low
    half = slice(2 * depth, 3 * depth)
    half_back[...] = jnp.concatenate([back_high[:, half], back_low[:, half], back_high[:, half]], axis=1)
    high, low = split(matrix)
    depth_high, depth_low = high[:, :padded], low[:, :padded]

    flip_x, flip_y = is_odd("gx"), is_odd("gy")
    for e in range(rows + 2 * side):
        if e < side:
            extended[e, 0:depth] = jnp.where(flip_x, even_x[e], odd_x[e])
        elif e < side + rows:
            extended[e, 0:depth] = own[:, e - side]
        else:
            extended[e, 0:depth] = jnp.where(flip_x, odd_x[e - side - rows], even_x[e - side - rows])
        even, odd = even_y[e * reach : (e + 1) * reach], odd_y[e * reach : (e + 1) * reach]
        extended[e, depth : depth + reach] = jnp.where(flip_y, even, odd)
        extended[e, depth + reach : deep] = jnp.where(flip_y, odd, even)
        if padded > deep:
            extended[e, deep:padded] = jnp.zeros((padded - deep, lanes), F32)

    for i in range(rows + 2 * side):
        e_high, e_low = split(extended[i])
        blurred[i] = dot(depth_high, e_high) + dot(depth_high, e_low) + dot(depth_low, e_high)

    inward = lax.broadcasted_iota(jnp.int32, (lanes, lanes), 0)
    outward = lax.broadcasted_iota(jnp.int32, (lanes, lanes), 1)
    for turn, view in enumerate(views):
        place = outward
        if turn % 2 == 0:
            place = outward - offsets[view]
            place = jnp.where(place < 0, place + lanes, place)
        tap = (lanes - 1 - place - inward if turn >= 2 else inward - place) + side
        source = row_taps if turn % 2 else column_taps
        matrix = jnp.zeros((lanes, lanes), F32)
        for r in range(width):
            matrix = jnp.where(tap == r, source[view, r], matrix)
        high, low = split(matrix)
        back_high, back_low = split(matrix.T)
        lane_back[turn, 0] = back_high
        lane_back[turn, 1] = back_low
        both = jnp.concatenate([high, high], axis=0)
        factor = row_taps_of(turn, view, row_taps, column_taps, width)
        for i in range(rows):
            layers = pl.ds(turn * depth, depth)
            total = factor[0] * blurred[i, layers]
            for s in range(1, width):
                total = total + factor[s] * blurred[i + s, layers]
            t_high, t_low = split(total)
            predicted[turn, i] = dot(jnp.concatenate([t_high, t_low], axis=1), both) + dot(t_high, low)


def turned(mine, swapped, received, arrived, data):
    parts, _, rows, wide = arrived.shape
    group = LANES // rows
    me = lax.axis_index("gx")
    for k in range(parts // 2):
        for core in range(2):
            source = lax.bitwise_xor(me, 2 * k + core)
            if k > 0:
                arrived[source] = received[k - 1][core]
            else:
                arrived[source] = swapped[0] if core else mine[0]
    granule = lax.broadcasted_iota(jnp.int32, (8, LANES), 1) // rows
    for slot in range(2):
        for part in range(0, parts, group):
            for eight in range(0, rows, 8):
                for piece in range(wide // LANES):
                    held = [
                        arrived[part + s, slot, eight : eight + 8, piece * LANES : (piece + 1) * LANES]
                        for s in range(group)
                    ]
                    step = 1
                    while step < group:
                        upper = (granule // step) % 2 == 1
                        crossed = list(held)
                        for s in range(group):
                            if s & step == 0:
                                one, two = held[s], held[s + step]
                                crossed[s] = jnp.where(upper, pltpu.roll(two, step * rows, 1), one)
                                crossed[s + step] = jnp.where(upper, two, pltpu.roll(one, LANES - step * rows, 1))
                        held = crossed
                        step *= 2
                    for s in range(group):
                        data[slot, eight : eight + 8, piece * group + s, part * rows : part * rows + LANES] = held[s]


def lane_blur(recorded, predicted, back):
    high, low = back[0], back[1]
    r_high, r_low = split(recorded / predicted)
    both = jnp.concatenate([high, high], axis=0)
    return dot(jnp.concatenate([r_high, r_low], axis=1), both) + dot(r_high, low)


def depth_blur(back, parts):
    high, low = back[0], back[1]
    s_high, s_low = split(jnp.concatenate(parts, axis=0))
    both = jnp.concatenate([high, low], axis=1)
    return dot(both, jnp.concatenate([s_high, s_high], axis=0)) + dot(high, s_low)


def spread_row(e, factor, places, backed):
    total = None
    for i, place in places.items():
        if 0 <= e - i < len(factor):
            term = factor[e - i] * backed[place]
            total = term if total is None else total + term
    return jnp.zeros(backed.shape[1:], F32) if total is None else total


def project_sides(turns, row_taps, column_taps, predicted, lane_back, depth_back, kept, outer, mine, swapped, *rest):
    received, (even_pair, odd_pair, data, backed, arrived) = rest[:-5], rest[-5:]
    _, rows, depth, lanes = predicted.shape
    side, deep, _ = even_pair.shape
    turned(mine, swapped, received, arrived, data)
    row_list = [*range(side), *range(rows - side, rows)]
    for turn in range(VIEWS):
        for j, i in enumerate(row_list):
            if turn == 0:
                recorded = kept[:, i]
            elif turn == 2:
                recorded = outer[:, 2 * side - 1 - j]
            else:
                recorded = data[turn // 2, rows - 1 - i if turn == 1 else i]
            backed[turn, j] = lane_blur(recorded, predicted[turn, i], lane_back.at[turn])
    factors = [
        row_taps_of(turn, view_of(turns, turn), row_taps, column_taps, 2 * side + 1) for turn in range(VIEWS)
    ]
    places = {i: j for j, i in enumerate(row_list)}
    results = [
        depth_blur(depth_back, [spread_row(e, factors[turn], places, backed.at[turn]) for turn in range(VIEWS)])[:deep]
        for e in [*range(side), *range(rows + side, rows + 2 * side)]
    ]
    odd = is_odd("gx")
    for i in range(side):
        first, last = results[i], results[side + i]
        even_pair[i] = jnp.where(odd, first, last)
        odd_pair[i] = jnp.where(odd, last, first)


def project(turns, row_taps, column_taps, predicted, lane_back, depth_back, kept, data, outer_backed, middle, backed):
    _, rows, depth, lanes = predicted.shape
    deep = middle.shape[1]
    side = outer_backed.shape[1] // 2
    row_list = [*range(side), *range(rows - side, rows)]
    for turn in range(VIEWS):
        for j, i in enumerate(row_list):
            backed[turn, i] = outer_backed[turn, j]
        for i in range(side, rows - side):
            if turn == 0:
                recorded = kept[:, i]
            elif turn == 2:
                continue
            else:
                recorded = data[turn // 2, rows - 1 - i if turn == 1 else i]
            backed[turn, i] = lane_blur(recorded, predicted[turn, i], lane_back.at[turn])
    factors = [
        row_taps_of(turn, view_of(turns, turn), row_taps, column_taps, 2 * side + 1) for turn in range(VIEWS)
    ]
    every, half = {i: i for i in range(rows)}, {i: i for i in row_list}
    for e in range(rows):
        parts = [
            spread_row(e + side, factors[turn], half if turn == 2 else every, backed.at[turn]) for turn in range(VIEWS)
        ]
        middle[e] = depth_blur(depth_back, parts)[:deep]


def project_half(turns, row_taps, column_taps, predicted, lane_back, half_back, flat, partial, middle, backed, inner):
    _, rows, depth, lanes = predicted.shape
    deep = middle.shape[1]
    side = (rows - inner.shape[1]) // 2
    inner[...] = flat[: depth * inner.shape[1]].reshape(inner.shape)
    row_list = range(side, rows - side)
    for i in row_list:
        backed[i] = lane_blur(inner[:, rows - side - 1 - i], predicted[2, i], lane_back.at[2])
    factor = row_taps_of(2, view_of(turns, 2), row_taps, column_taps, 2 * side + 1)
    back = half_back[...]
    for e in range(rows):
        s_high, s_low = split(spread_row(e + side, factor, {i: i for i in row_list}, backed))
        result = dot(back, jnp.concatenate([s_high, s_high, s_low], axis=0))
        middle[e] = partial[e] + result[:deep]


def gather_sides(middle, even_x, odd_x, own, even_pair, odd_pair):
    rows = middle.shape[0]
    side = even_x.shape[0]
    depth = own.shape[1]
    reach = even_pair.shape[0] // rows
    flip_x, flip_y = is_odd("gx"), is_odd("gy")
    for i in range(rows):
        value = middle[i]
        if i < side:
            value = value + jnp.where(flip_x, even_x[i], odd_x[i])
        if i >= rows - side:
            j = i - rows + side
            value = value + jnp.where(flip_x, odd_x[j], even_x[j])
        own[i] = value[:depth]
        before, after = value[depth : depth + reach], value[depth + reach : depth + 2 * reach]
        even_pair[i * reach : (i + 1) * reach] = jnp.where(flip_y, before, after)
        odd_pair[i * reach : (i + 1) * reach] = jnp.where(flip_y, after, before)


def finish(estimate, own, even_y, odd_y, out):
    rows, depth, lanes = own.shape
    reach = even_y.shape[0] // rows
    flip_y = is_odd("gy")
    rest = jnp.zeros((depth - reach, lanes), F32)
    for i in range(rows):
        even, odd = even_y[i * reach : (i + 1) * reach], odd_y[i * reach : (i + 1) * reach]
        first, last = jnp.where(flip_y, even, odd), jnp.where(flip_y, odd, even)
        value = own[i] + jnp.concatenate([first, rest], axis=0) + jnp.concatenate([rest, last], axis=0)
        out[:, i] = estimate[:, i] * value * (1.0 / VIEWS)


def call(body, out_shape, specs, scratch=()):
    return pl.pallas_call(
        body,
        out_shape=out_shape,
        in_specs=specs,
        out_specs=jax.tree.map(lambda _: VMEM, out_shape),
        scratch_shapes=scratch,
        compiler_params=PARAMS,
        cost_estimate=COST,
    )


def shards(estimate, recorded, quarter_turns, offsets, depth_taps, row_taps, column_taps):
    depth, rows, lanes = estimate.shape
    reach = (depth_taps.shape[1] - 1) // 2
    side = (row_taps.shape[1] - 1) // 2
    deep = depth + 2 * reach
    padded = -(-deep // 16) * 16
    parts = lax.axis_size("gx")
    even_y, odd_y = pairs(lax.axis_size("gy"))
    even_x, odd_x = pairs(parts)

    wide, chips = depth * rows, parts // 2
    edge, second = call(edges, (struct(side, depth, lanes),) * 2, [VMEM])(estimate)
    first, second = lax.ppermute(edge, "gx", even_x), lax.ppermute(second, "gx", odd_x)
    kept, mine, theirs = call(
        prepare,
        (struct(depth, rows, lanes),) + (struct(chips, 2, rows, wide),) * 2,
        [SMEM, SMEM, VMEM, ORDER],
        [pltpu.VMEM((lanes, wide), F32)],
    )(quarter_turns, offsets, recorded, first)
    mirror = [(i, parts - 1 - i) for i in range(parts)]
    swapped = lax.ppermute(theirs, "gx", [(i, i ^ 1) for i in range(parts)])
    messages = call(merge, (struct(2, 2, rows, wide),) * (chips - 1), [VMEM] * 2)(mine, swapped)
    outer, inner = pl.pallas_call(
        pick,
        out_shape=(struct(depth, 2 * side, lanes), struct(depth, rows - 2 * side, lanes)),
        grid_spec=pltpu.PrefetchScalarGridSpec(
            num_scalar_prefetch=1,
            grid=(1,),
            in_specs=[
                pl.BlockSpec((1, depth, rows, lanes), lambda i, turns: (view_of(turns, 2), 0, 0, 0)),
                ORDER,
            ],
            out_specs=[
                pl.BlockSpec((depth, 2 * side, lanes), lambda i, turns: (0, 0, 0)),
                pl.BlockSpec((depth, rows - 2 * side, lanes), lambda i, turns: (0, 0, 0)),
            ],
        ),
        compiler_params=PARAMS,
        cost_estimate=COST,
    )(quarter_turns, recorded, messages[0])
    outer = lax.ppermute(outer, "gx", mirror)
    third, fourth = call(layers_out, (struct((rows + 2 * side) * reach, lanes),) * 2, [VMEM] * 3)(estimate, first, second)
    third, fourth = lax.ppermute(third, "gy", even_y), lax.ppermute(fourth, "gy", odd_y)
    moved = {
        k: lax.ppermute(messages[k - 1], "gx", [(i, i ^ (2 * k)) for i in range(parts)])
        for k in range(chips - 1, 0, -1)
    }

    predicted, lane_back, depth_back, half_back = call(
        predict,
        (
            struct(VIEWS, rows, depth, lanes),
            struct(VIEWS, 2, lanes, lanes, dtype=BF16),
            struct(2, padded, VIEWS * depth, dtype=BF16),
            struct(padded, 3 * depth, dtype=BF16),
        ),
        [SMEM] * 5 + [VMEM] * 5,
        [
            pltpu.VMEM((rows + 2 * side, padded, lanes), F32),
            pltpu.VMEM((rows + 2 * side, VIEWS * depth, lanes), F32),
        ],
    )(quarter_turns, offsets, depth_taps, row_taps, column_taps, estimate, first, second, third, fourth)

    inner = call(hold, struct(side * deep + 8, lanes), [VMEM] + [ORDER] * (chips + 1))(inner, predicted, outer, *moved.values())
    inner = lax.ppermute(inner, "gx", mirror)
    first, second, data, backed = call(
        project_sides,
        (struct(side, deep, lanes),) * 2 + (struct(2, rows, depth, lanes), struct(VIEWS, 2 * side, depth, lanes)),
        [SMEM] * 3 + [VMEM] * (6 + chips),
        [pltpu.VMEM((parts, 2, rows, wide), F32)],
    )(quarter_turns, row_taps, column_taps, predicted, lane_back, depth_back, kept, outer, mine, swapped,
      *[moved[k] for k in range(1, chips)])
    first, second = lax.ppermute(first, "gx", even_x), lax.ppermute(second, "gx", odd_x)
    middle = call(
        project,
        struct(rows, deep, lanes),
        [SMEM] * 3 + [VMEM] * 6,
        [pltpu.VMEM((VIEWS, rows, depth, lanes), F32)],
    )(quarter_turns, row_taps, column_taps, predicted, lane_back, depth_back, kept, data, backed)
    middle = call(
        project_half,
        struct(rows, deep, lanes),
        [SMEM] * 3 + [VMEM] * 5,
        [pltpu.VMEM((rows, depth, lanes), F32), pltpu.VMEM((depth, rows - 2 * side, lanes), F32)],
    )(quarter_turns, row_taps, column_taps, predicted, lane_back, half_back, inner, middle)
    own, third, fourth = call(
        gather_sides,
        (struct(rows, depth, lanes), struct(rows * reach, lanes), struct(rows * reach, lanes)),
        [VMEM] * 3,
    )(middle, first, second)
    third, fourth = lax.ppermute(third, "gy", even_y), lax.ppermute(fourth, "gy", odd_y)
    return call(finish, struct(depth, rows, lanes), [VMEM] * 4)(estimate, own, third, fourth)


def solution(mesh):
    in_specs = (P("gy", "gx", None), P(None, "gy", "gx", None), P(), P(), P(), P(), P())
    out_specs = P("gy", "gx", None)
    return jax.shard_map(shards, mesh=mesh, in_specs=in_specs, out_specs=out_specs, check_vma=False)
```

```python
import functools

import jax
import jax.numpy as jnp
from jax import lax
from jax.experimental import pallas as pl
from jax.experimental.pallas import tpu as pltpu
from jax.sharding import PartitionSpec as P

VIEWS = 4
LANES = 128
VMEM = pl.BlockSpec(memory_space=pltpu.VMEM)
ORDER = pl.BlockSpec(memory_space=pl.ANY)
SMEM = pl.BlockSpec(memory_space=pltpu.SMEM)
PARAMS = pltpu.CompilerParams(vmem_limit_bytes=24 * 1024 * 1024)
F32 = jnp.float32
BF16 = jnp.bfloat16
COST = pl.CostEstimate(flops=1, bytes_accessed=1, transcendentals=0)


def struct(*shape, dtype=F32):
    return jax.ShapeDtypeStruct(shape, dtype)


def view_of(turns_ref, turn):
    found = jnp.int32(0)
    for view in range(1, VIEWS):
        found = jnp.where(turns_ref[view] == turn, jnp.int32(view), found)
    return found


def split(value):
    high = value.astype(BF16)
    return high, (value - high.astype(F32)).astype(BF16)


def dot(left, right):
    return jnp.dot(left, right, preferred_element_type=F32)


def pairs(width):
    def swaps(initial):
        return [p for i in range(initial, width - 1, 2) for p in ((i, i + 1), (i + 1, i))]

    return swaps(0), swaps(1)


def is_odd(axis):
    return lax.rem(lax.axis_index(axis), 2) == 1


def pick(turns, recorded, later, outer, inner):
    rows = recorded.shape[2]
    half = outer.shape[1] // 2
    outer[:, :half] = recorded[0, :, :half]
    outer[:, half:] = recorded[0, :, rows - half :]
    inner[...] = recorded[0, :, half : rows - half]


def prepare(turns, offsets, recorded, later, kept, mine, theirs, across):
    depth, rows, lanes = recorded.shape[1:]
    chips, _, _, wide = mine.shape
    me = lax.axis_index("gx")
    kept[...] = recorded[view_of(turns, 0)]
    for slot, turn in enumerate((1, 3)):
        view = view_of(turns, turn)
        volume = recorded[view].reshape(depth * rows, lanes)
        volume = pltpu.roll(volume, lax.rem(lanes - offsets[view], lanes), 1)
        across[...] = volume.T
        for k in range(2 * chips):
            to = lax.bitwise_xor(me, k)
            part = 2 * chips - 1 - to if turn == 1 else to
            block = across[pl.ds(pl.multiple_of(part * rows, rows), rows)]
            if k % 2 == 0:
                mine[k // 2, slot] = block
            else:
                theirs[k // 2, slot] = block


def merge(mine, swapped, *outs):
    for k in range(1, mine.shape[0]):
        for slot in range(2):
            outs[k - 1][0, slot] = mine[k, slot]
            outs[k - 1][1, slot] = swapped[k, slot]


def hold(inner, *rest):
    flat = rest[-1]
    depth, count, lanes = inner.shape
    flat[: depth * count] = inner[...].reshape(depth * count, lanes)
    flat[depth * count :] = jnp.zeros((flat.shape[0] - depth * count, lanes), F32)


def edges(own, even_pair, odd_pair):
    rows = own.shape[1]
    side = even_pair.shape[0]
    odd = is_odd("gx")
    for i in range(side):
        first, last = own[:, i], own[:, rows - side + i]
        even_pair[i] = jnp.where(odd, first, last)
        odd_pair[i] = jnp.where(odd, last, first)


def layers_out(own, from_even, from_odd, even_pair, odd_pair):
    depth, rows, _ = own.shape
    side = from_even.shape[0]
    reach = even_pair.shape[0] // (rows + 2 * side)
    odd_x, odd_y = is_odd("gx"), is_odd("gy")
    for e in range(rows + 2 * side):
        if e < side:
            value = jnp.where(odd_x, from_even[e], from_odd[e])
        elif e < side + rows:
            value = own[:, e - side]
        else:
            value = jnp.where(odd_x, from_odd[e - side - rows], from_even[e - side - rows])
        first, last = value[:reach], value[depth - reach :]
        even_pair[e * reach : (e + 1) * reach] = jnp.where(odd_y, first, last)
        odd_pair[e * reach : (e + 1) * reach] = jnp.where(odd_y, last, first)


def row_taps_of(turn, view, row_taps, column_taps, width):
    source = column_taps if turn % 2 else row_taps
    flipped = turn in (1, 2)
    return [source[view, width - 1 - s if flipped else s] for s in range(width)]


def predict(turns, offsets, depth_taps, row_taps, column_taps, own, even_x, odd_x, even_y, odd_y, later,
            predicted, lane_back, depth_back, half_back, extended, blurred):
    depth, rows, lanes = own.shape
    side = even_x.shape[0]
    reach = even_y.shape[0] // (rows + 2 * side)
    width = 2 * side + 1
    deep = depth + 2 * reach
    padded = extended.shape[1]
    views = [view_of(turns, turn) for turn in range(VIEWS)]

    column = lax.broadcasted_iota(jnp.int32, (depth, LANES), 1)
    row = lax.broadcasted_iota(jnp.int32, (depth, LANES), 0)
    layer = jnp.where(column < depth, column, jnp.where(column < depth + reach, column - depth - reach, column - reach))
    tap = jnp.where(column < deep, layer - row + reach, -1)
    stacked = []
    for view in views:
        matrix = jnp.zeros((depth, LANES), F32)
        for t in range(2 * reach + 1):
            matrix = jnp.where(tap == t, depth_taps[view, t], matrix)
        stacked.append(matrix)
    matrix = jnp.concatenate(stacked, axis=0)
    back_high, back_low = split(matrix.T[:padded])
    depth_back[0] = back_high
    depth_back[1] = back_low
    half = slice(2 * depth, 3 * depth)
    half_back[...] = jnp.concatenate([back_high[:, half], back_low[:, half], back_high[:, half]], axis=1)
    high, low = split(matrix)
    depth_high, depth_low = high[:, :padded], low[:, :padded]

    flip_x, flip_y = is_odd("gx"), is_odd("gy")
    for e in range(rows + 2 * side):
        if e < side:
            extended[e, 0:depth] = jnp.where(flip_x, even_x[e], odd_x[e])
        elif e < side + rows:
            extended[e, 0:depth] = own[:, e - side]
        else:
            extended[e, 0:depth] = jnp.where(flip_x, odd_x[e - side - rows], even_x[e - side - rows])
        even, odd = even_y[e * reach : (e + 1) * reach], odd_y[e * reach : (e + 1) * reach]
        extended[e, depth : depth + reach] = jnp.where(flip_y, even, odd)
        extended[e, depth + reach : deep] = jnp.where(flip_y, odd, even)
        if padded > deep:
            extended[e, deep:padded] = jnp.zeros((padded - deep, lanes), F32)

    for i in range(rows + 2 * side):
        e_high, e_low = split(extended[i])
        blurred[i] = dot(depth_high, e_high) + dot(depth_high, e_low) + dot(depth_low, e_high)

    inward = lax.broadcasted_iota(jnp.int32, (lanes, lanes), 0)
    outward = lax.broadcasted_iota(jnp.int32, (lanes, lanes), 1)
    for turn, view in enumerate(views):
        place = outward
        if turn % 2 == 0:
            place = outward - offsets[view]
            place = jnp.where(place < 0, place + lanes, place)
        tap = (lanes - 1 - place - inward if turn >= 2 else inward - place) + side
        source = row_taps if turn % 2 else column_taps
        matrix = jnp.zeros((lanes, lanes), F32)
        for r in range(width):
            matrix = jnp.where(tap == r, source[view, r], matrix)
        high, low = split(matrix)
        back_high, back_low = split(matrix.T)
        lane_back[turn, 0] = back_high
        lane_back[turn, 1] = back_low
        both = jnp.concatenate([high, high], axis=0)
        factor = row_taps_of(turn, view, row_taps, column_taps, width)
        for i in range(rows):
            layers = pl.ds(turn * depth, depth)
            total = factor[0] * blurred[i, layers]
            for s in range(1, width):
                total = total + factor[s] * blurred[i + s, layers]
            t_high, t_low = split(total)
            predicted[turn, i] = dot(jnp.concatenate([t_high, t_low], axis=1), both) + dot(t_high, low)


def gate(*rest):
    rest[-1][...] = jnp.zeros(rest[-1].shape, F32)


def turned(mine, swapped, *rest):
    received, (data, arrived) = rest[:-2], rest[-2:]
    parts, _, rows, wide = arrived.shape
    group = LANES // rows
    me = lax.axis_index("gx")
    for k in range(parts // 2):
        for core in range(2):
            source = lax.bitwise_xor(me, 2 * k + core)
            if k > 0:
                arrived[source] = received[k - 1][core]
            else:
                arrived[source] = swapped[0] if core else mine[0]
    granule = lax.broadcasted_iota(jnp.int32, (8, LANES), 1) // rows
    for slot in range(2):
        for part in range(0, parts, group):
            for eight in range(0, rows, 8):
                for piece in range(wide // LANES):
                    held = [
                        arrived[part + s, slot, eight : eight + 8, piece * LANES : (piece + 1) * LANES]
                        for s in range(group)
                    ]
                    step = 1
                    while step < group:
                        upper = (granule // step) % 2 == 1
                        crossed = list(held)
                        for s in range(group):
                            if s & step == 0:
                                one, two = held[s], held[s + step]
                                crossed[s] = jnp.where(upper, pltpu.roll(two, step * rows, 1), one)
                                crossed[s + step] = jnp.where(upper, two, pltpu.roll(one, LANES - step * rows, 1))
                        held = crossed
                        step *= 2
                    for s in range(group):
                        data[slot, eight : eight + 8, piece * group + s, part * rows : part * rows + LANES] = held[s]


def lane_blur(recorded, predicted, back):
    high, low = back[0], back[1]
    r_high, r_low = split(recorded / predicted)
    both = jnp.concatenate([high, high], axis=0)
    return dot(jnp.concatenate([r_high, r_low], axis=1), both) + dot(r_high, low)


def depth_blur(back, parts):
    high, low = back[0], back[1]
    s_high, s_low = split(jnp.concatenate(parts, axis=0))
    both = jnp.concatenate([high, low], axis=1)
    return dot(both, jnp.concatenate([s_high, s_high], axis=0)) + dot(high, s_low)


def spread_row(e, factor, places, backed):
    total = None
    for i, place in places.items():
        if 0 <= e - i < len(factor):
            term = factor[e - i] * backed[place]
            total = term if total is None else total + term
    return jnp.zeros(backed.shape[1:], F32) if total is None else total


def project_sides(turns, row_taps, column_taps, predicted, lane_back, depth_back, kept, outer, data, even_pair, odd_pair, backed):
    _, rows, depth, lanes = predicted.shape
    side, deep, _ = even_pair.shape
    row_list = [*range(side), *range(rows - side, rows)]
    for turn in range(VIEWS):
        for j, i in enumerate(row_list):
            if turn == 0:
                recorded = kept[:, i]
            elif turn == 2:
                recorded = outer[:, 2 * side - 1 - j]
            else:
                recorded = data[turn // 2, rows - 1 - i if turn == 1 else i]
            backed[turn, j] = lane_blur(recorded, predicted[turn, i], lane_back.at[turn])
    factors = [
        row_taps_of(turn, view_of(turns, turn), row_taps, column_taps, 2 * side + 1) for turn in range(VIEWS)
    ]
    places = {i: j for j, i in enumerate(row_list)}
    results = [
        depth_blur(depth_back, [spread_row(e, factors[turn], places, backed.at[turn]) for turn in range(VIEWS)])[:deep]
        for e in [*range(side), *range(rows + side, rows + 2 * side)]
    ]
    odd = is_odd("gx")
    for i in range(side):
        first, last = results[i], results[side + i]
        even_pair[i] = jnp.where(odd, first, last)
        odd_pair[i] = jnp.where(odd, last, first)


def project(turns, row_taps, column_taps, predicted, lane_back, depth_back, kept, data, outer_backed, middle, backed):
    _, rows, depth, lanes = predicted.shape
    deep = middle.shape[1]
    side = outer_backed.shape[1] // 2
    row_list = [*range(side), *range(rows - side, rows)]
    for turn in range(VIEWS):
        for j, i in enumerate(row_list):
            backed[turn, i] = outer_backed[turn, j]
        for i in range(side, rows - side):
            if turn == 0:
                recorded = kept[:, i]
            elif turn == 2:
                continue
            else:
                recorded = data[turn // 2, rows - 1 - i if turn == 1 else i]
            backed[turn, i] = lane_blur(recorded, predicted[turn, i], lane_back.at[turn])
    factors = [
        row_taps_of(turn, view_of(turns, turn), row_taps, column_taps, 2 * side + 1) for turn in range(VIEWS)
    ]
    every, half = {i: i for i in range(rows)}, {i: i for i in row_list}
    for e in range(rows):
        parts = [
            spread_row(e + side, factors[turn], half if turn == 2 else every, backed.at[turn]) for turn in range(VIEWS)
        ]
        middle[e] = depth_blur(depth_back, parts)[:deep]


def project_half(turns, row_taps, column_taps, predicted, lane_back, half_back, flat, partial, middle, backed, inner):
    _, rows, depth, lanes = predicted.shape
    deep = middle.shape[1]
    side = (rows - inner.shape[1]) // 2
    inner[...] = flat[: depth * inner.shape[1]].reshape(inner.shape)
    row_list = range(side, rows - side)
    for i in row_list:
        backed[i] = lane_blur(inner[:, rows - side - 1 - i], predicted[2, i], lane_back.at[2])
    factor = row_taps_of(2, view_of(turns, 2), row_taps, column_taps, 2 * side + 1)
    back = half_back[...]
    for e in range(rows):
        s_high, s_low = split(spread_row(e + side, factor, {i: i for i in row_list}, backed))
        result = dot(back, jnp.concatenate([s_high, s_high, s_low], axis=0))
        middle[e] = partial[e] + result[:deep]


def gather_sides(middle, even_x, odd_x, own, even_pair, odd_pair):
    rows = middle.shape[0]
    side = even_x.shape[0]
    depth = own.shape[1]
    reach = even_pair.shape[0] // rows
    flip_x, flip_y = is_odd("gx"), is_odd("gy")
    for i in range(rows):
        value = middle[i]
        if i < side:
            value = value + jnp.where(flip_x, even_x[i], odd_x[i])
        if i >= rows - side:
            j = i - rows + side
            value = value + jnp.where(flip_x, odd_x[j], even_x[j])
        own[i] = value[:depth]
        before, after = value[depth : depth + reach], value[depth + reach : depth + 2 * reach]
        even_pair[i * reach : (i + 1) * reach] = jnp.where(flip_y, before, after)
        odd_pair[i * reach : (i + 1) * reach] = jnp.where(flip_y, after, before)


def finish(estimate, own, even_y, odd_y, out):
    rows, depth, lanes = own.shape
    reach = even_y.shape[0] // rows
    flip_y = is_odd("gy")
    rest = jnp.zeros((depth - reach, lanes), F32)
    for i in range(rows):
        even, odd = even_y[i * reach : (i + 1) * reach], odd_y[i * reach : (i + 1) * reach]
        first, last = jnp.where(flip_y, even, odd), jnp.where(flip_y, odd, even)
        value = own[i] + jnp.concatenate([first, rest], axis=0) + jnp.concatenate([rest, last], axis=0)
        out[:, i] = estimate[:, i] * value * (1.0 / VIEWS)


def call(body, out_shape, specs, scratch=()):
    return pl.pallas_call(
        body,
        out_shape=out_shape,
        in_specs=specs,
        out_specs=jax.tree.map(lambda _: VMEM, out_shape),
        scratch_shapes=scratch,
        compiler_params=PARAMS,
        cost_estimate=COST,
    )


def shards(estimate, recorded, quarter_turns, offsets, depth_taps, row_taps, column_taps):
    depth, rows, lanes = estimate.shape
    reach = (depth_taps.shape[1] - 1) // 2
    side = (row_taps.shape[1] - 1) // 2
    deep = depth + 2 * reach
    padded = -(-deep // 16) * 16
    parts = lax.axis_size("gx")
    even_y, odd_y = pairs(lax.axis_size("gy"))
    even_x, odd_x = pairs(parts)

    wide, chips = depth * rows, parts // 2
    edge, second = call(edges, (struct(side, depth, lanes),) * 2, [VMEM])(estimate)
    first, second = lax.ppermute(edge, "gx", even_x), lax.ppermute(second, "gx", odd_x)
    kept, mine, theirs = call(
        prepare,
        (struct(depth, rows, lanes),) + (struct(chips, 2, rows, wide),) * 2,
        [SMEM, SMEM, VMEM, ORDER],
        [pltpu.VMEM((lanes, wide), F32)],
    )(quarter_turns, offsets, recorded, first)
    mirror = [(i, parts - 1 - i) for i in range(parts)]
    swapped = lax.ppermute(theirs, "gx", [(i, i ^ 1) for i in range(parts)])
    messages = call(merge, (struct(2, 2, rows, wide),) * (chips - 1), [VMEM] * 2)(mine, swapped)
    outer, inner = pl.pallas_call(
        pick,
        out_shape=(struct(depth, 2 * side, lanes), struct(depth, rows - 2 * side, lanes)),
        grid_spec=pltpu.PrefetchScalarGridSpec(
            num_scalar_prefetch=1,
            grid=(1,),
            in_specs=[
                pl.BlockSpec((1, depth, rows, lanes), lambda i, turns: (view_of(turns, 2), 0, 0, 0)),
                ORDER,
            ],
            out_specs=[
                pl.BlockSpec((depth, 2 * side, lanes), lambda i, turns: (0, 0, 0)),
                pl.BlockSpec((depth, rows - 2 * side, lanes), lambda i, turns: (0, 0, 0)),
            ],
        ),
        compiler_params=PARAMS,
        cost_estimate=COST,
    )(quarter_turns, recorded, messages[0])
    outer = lax.ppermute(outer, "gx", mirror)
    third, fourth = call(layers_out, (struct((rows + 2 * side) * reach, lanes),) * 2, [VMEM] * 3)(estimate, first, second)
    third, fourth = lax.ppermute(third, "gy", even_y), lax.ppermute(fourth, "gy", odd_y)
    moved = {
        k: lax.ppermute(messages[k - 1], "gx", [(i, i ^ (2 * k)) for i in range(parts)])
        for k in range(chips - 1, 0, -1)
    }

    arrivals = list(moved.values())
    passed = call(gate, struct(8, LANES), [ORDER] * len(arrivals))(*arrivals)
    data = call(
        turned,
        struct(2, rows, depth, lanes),
        [VMEM] * (1 + chips),
        [pltpu.VMEM((parts, 2, rows, wide), F32)],
    )(mine, swapped, *[moved[k] for k in range(1, chips)])

    predicted, lane_back, depth_back, half_back = call(
        predict,
        (
            struct(VIEWS, rows, depth, lanes),
            struct(VIEWS, 2, lanes, lanes, dtype=BF16),
            struct(2, padded, VIEWS * depth, dtype=BF16),
            struct(padded, 3 * depth, dtype=BF16),
        ),
        [SMEM] * 5 + [VMEM] * 5 + [ORDER],
        [
            pltpu.VMEM((rows + 2 * side, padded, lanes), F32),
            pltpu.VMEM((rows + 2 * side, VIEWS * depth, lanes), F32),
        ],
    )(quarter_turns, offsets, depth_taps, row_taps, column_taps, estimate, first, second, third, fourth, passed)

    inner = call(hold, struct(side * deep + 8, lanes), [VMEM] + [ORDER] * 2)(inner, predicted, outer)
    inner = lax.ppermute(inner, "gx", mirror)
    first, second, backed = call(
        project_sides,
        (struct(side, deep, lanes),) * 2 + (struct(VIEWS, 2 * side, depth, lanes),),
        [SMEM] * 3 + [VMEM] * 6,
    )(quarter_turns, row_taps, column_taps, predicted, lane_back, depth_back, kept, outer, data)
    first, second = lax.ppermute(first, "gx", even_x), lax.ppermute(second, "gx", odd_x)
    middle = call(
        project,
        struct(rows, deep, lanes),
        [SMEM] * 3 + [VMEM] * 6,
        [pltpu.VMEM((VIEWS, rows, depth, lanes), F32)],
    )(quarter_turns, row_taps, column_taps, predicted, lane_back, depth_back, kept, data, backed)
    middle = call(
        project_half,
        struct(rows, deep, lanes),
        [SMEM] * 3 + [VMEM] * 5,
        [pltpu.VMEM((rows, depth, lanes), F32), pltpu.VMEM((depth, rows - 2 * side, lanes), F32)],
    )(quarter_turns, row_taps, column_taps, predicted, lane_back, half_back, inner, middle)
    own, third, fourth = call(
        gather_sides,
        (struct(rows, depth, lanes), struct(rows * reach, lanes), struct(rows * reach, lanes)),
        [VMEM] * 3,
    )(middle, first, second)
    third, fourth = lax.ppermute(third, "gy", even_y), lax.ppermute(fourth, "gy", odd_y)
    return call(finish, struct(depth, rows, lanes), [VMEM] * 4)(estimate, own, third, fourth)


def solution(mesh):
    in_specs = (P("gy", "gx", None), P(None, "gy", "gx", None), P(), P(), P(), P(), P())
    out_specs = P("gy", "gx", None)
    return jax.shard_map(shards, mesh=mesh, in_specs=in_specs, out_specs=out_specs, check_vma=False)
```

```python
import functools

import jax
import jax.numpy as jnp
from jax import lax
from jax.experimental import pallas as pl
from jax.experimental.pallas import tpu as pltpu
from jax.sharding import PartitionSpec as P

VIEWS = 4
LANES = 128
VMEM = pl.BlockSpec(memory_space=pltpu.VMEM)
ORDER = pl.BlockSpec(memory_space=pl.ANY)
SMEM = pl.BlockSpec(memory_space=pltpu.SMEM)
PARAMS = pltpu.CompilerParams(vmem_limit_bytes=24 * 1024 * 1024)
F32 = jnp.float32
BF16 = jnp.bfloat16
COST = pl.CostEstimate(flops=1, bytes_accessed=1, transcendentals=0)


def struct(*shape, dtype=F32):
    return jax.ShapeDtypeStruct(shape, dtype)


def view_of(turns_ref, turn):
    found = jnp.int32(0)
    for view in range(1, VIEWS):
        found = jnp.where(turns_ref[view] == turn, jnp.int32(view), found)
    return found


def split(value):
    high = value.astype(BF16)
    return high, (value - high.astype(F32)).astype(BF16)


def dot(left, right):
    return jnp.dot(left, right, preferred_element_type=F32)


def pairs(width):
    def swaps(initial):
        return [p for i in range(initial, width - 1, 2) for p in ((i, i + 1), (i + 1, i))]

    return swaps(0), swaps(1)


def is_odd(axis):
    return lax.rem(lax.axis_index(axis), 2) == 1


def pick(turns, recorded, later, later_too, outer, inner):
    rows = recorded.shape[2]
    half = outer.shape[1] // 2
    outer[:, :half] = recorded[0, :, :half]
    outer[:, half:] = recorded[0, :, rows - half :]
    inner[...] = recorded[0, :, half : rows - half]


def prepare(turns, offsets, recorded, later, kept, mine, theirs, across):
    depth, rows, lanes = recorded.shape[1:]
    chips, _, _, wide = mine.shape
    me = lax.axis_index("gx")
    kept[...] = recorded[view_of(turns, 0)]
    for slot, turn in enumerate((1, 3)):
        view = view_of(turns, turn)
        volume = recorded[view].reshape(depth * rows, lanes)
        volume = pltpu.roll(volume, lax.rem(lanes - offsets[view], lanes), 1)
        across[...] = volume.T
        for k in range(2 * chips):
            to = lax.bitwise_xor(me, k)
            part = 2 * chips - 1 - to if turn == 1 else to
            block = across[pl.ds(pl.multiple_of(part * rows, rows), rows)]
            if k % 2 == 0:
                mine[k // 2, slot] = block
            else:
                theirs[k // 2, slot] = block


def merge(mine, swapped, *outs):
    for k in range(1, mine.shape[0]):
        for slot in range(2):
            outs[k - 1][0, slot] = mine[k, slot]
            outs[k - 1][1, slot] = swapped[k, slot]


def hold(inner, *rest):
    flat = rest[-1]
    depth, count, lanes = inner.shape
    flat[: depth * count] = inner[...].reshape(depth * count, lanes)
    flat[depth * count :] = jnp.zeros((flat.shape[0] - depth * count, lanes), F32)


def edges(own, even_pair, odd_pair):
    rows = own.shape[1]
    side = even_pair.shape[0]
    odd = is_odd("gx")
    for i in range(side):
        first, last = own[:, i], own[:, rows - side + i]
        even_pair[i] = jnp.where(odd, first, last)
        odd_pair[i] = jnp.where(odd, last, first)


def layers_out(own, from_even, from_odd, even_pair, odd_pair):
    depth, rows, _ = own.shape
    side = from_even.shape[0]
    reach = even_pair.shape[0] // (rows + 2 * side)
    odd_x, odd_y = is_odd("gx"), is_odd("gy")
    for e in range(rows + 2 * side):
        if e < side:
            value = jnp.where(odd_x, from_even[e], from_odd[e])
        elif e < side + rows:
            value = own[:, e - side]
        else:
            value = jnp.where(odd_x, from_odd[e - side - rows], from_even[e - side - rows])
        first, last = value[:reach], value[depth - reach :]
        even_pair[e * reach : (e + 1) * reach] = jnp.where(odd_y, first, last)
        odd_pair[e * reach : (e + 1) * reach] = jnp.where(odd_y, last, first)


def row_taps_of(turn, view, row_taps, column_taps, width):
    source = column_taps if turn % 2 else row_taps
    flipped = turn in (1, 2)
    return [source[view, width - 1 - s if flipped else s] for s in range(width)]


def matrices(turns, offsets, depth_taps, row_taps, column_taps, depth_forth, lane_forth, depth_back, lane_back, half_back):
    padded = depth_back.shape[1]
    depth = half_back.shape[1] // 3
    lanes = lane_back.shape[2]
    reach = (depth_taps.shape[1] - 1) // 2
    width = row_taps.shape[1]
    deep = depth + 2 * reach
    views = [view_of(turns, turn) for turn in range(VIEWS)]
    column = lax.broadcasted_iota(jnp.int32, (depth, LANES), 1)
    row = lax.broadcasted_iota(jnp.int32, (depth, LANES), 0)
    layer = jnp.where(column < depth, column, jnp.where(column < depth + reach, column - depth - reach, column - reach))
    tap = jnp.where(column < deep, layer - row + reach, -1)
    stacked = []
    for view in views:
        matrix = jnp.zeros((depth, LANES), F32)
        for t in range(2 * reach + 1):
            matrix = jnp.where(tap == t, depth_taps[view, t], matrix)
        stacked.append(matrix)
    matrix = jnp.concatenate(stacked, axis=0)
    back_high, back_low = split(matrix.T[:padded])
    depth_back[0] = back_high
    depth_back[1] = back_low
    half = slice(2 * depth, 3 * depth)
    half_back[...] = jnp.concatenate([back_high[:, half], back_low[:, half], back_high[:, half]], axis=1)
    high, low = split(matrix)
    depth_forth[...] = jnp.concatenate([high[:, :padded], low[:, :padded], high[:, :padded]], axis=1)
    inward = lax.broadcasted_iota(jnp.int32, (lanes, lanes), 0)
    outward = lax.broadcasted_iota(jnp.int32, (lanes, lanes), 1)
    for turn, view in enumerate(views):
        place = outward
        if turn % 2 == 0:
            place = outward - offsets[view]
            place = jnp.where(place < 0, place + lanes, place)
        tap = (lanes - 1 - place - inward if turn >= 2 else inward - place) + width // 2
        source = row_taps if turn % 2 else column_taps
        matrix = jnp.zeros((lanes, lanes), F32)
        for r in range(width):
            matrix = jnp.where(tap == r, source[view, r], matrix)
        high, low = split(matrix)
        lane_forth[turn, 0] = high
        lane_forth[turn, 1] = low
        back_high, back_low = split(matrix.T)
        lane_back[turn, 0] = back_high
        lane_back[turn, 1] = back_low


def predict(turns, row_taps, column_taps, depth_forth, lane_forth, own, even_x, odd_x, even_y, odd_y, later,
            predicted, extended, blurred):
    depth, rows, lanes = own.shape
    side = even_x.shape[0]
    reach = even_y.shape[0] // (rows + 2 * side)
    width = 2 * side + 1
    deep = depth + 2 * reach
    padded = extended.shape[1]
    forth = depth_forth[...]

    flip_x, flip_y = is_odd("gx"), is_odd("gy")
    for e in range(rows + 2 * side):
        if e < side:
            extended[e, 0:depth] = jnp.where(flip_x, even_x[e], odd_x[e])
        elif e < side + rows:
            extended[e, 0:depth] = own[:, e - side]
        else:
            extended[e, 0:depth] = jnp.where(flip_x, odd_x[e - side - rows], even_x[e - side - rows])
        even, odd = even_y[e * reach : (e + 1) * reach], odd_y[e * reach : (e + 1) * reach]
        extended[e, depth : depth + reach] = jnp.where(flip_y, even, odd)
        extended[e, depth + reach : deep] = jnp.where(flip_y, odd, even)
        if padded > deep:
            extended[e, deep:padded] = jnp.zeros((padded - deep, lanes), F32)

    for i in range(0, rows + 2 * side, 2):
        e_high, e_low = split(jnp.concatenate([extended[i], extended[i + 1]], axis=1))
        result = dot(forth, jnp.concatenate([e_high, e_high, e_low], axis=0))
        blurred[i] = result[:, :lanes]
        blurred[i + 1] = result[:, lanes:]

    for turn in range(VIEWS):
        view = view_of(turns, turn)
        high, low = lane_forth[turn, 0], lane_forth[turn, 1]
        both = jnp.concatenate([high, high], axis=0)
        factor = row_taps_of(turn, view, row_taps, column_taps, width)
        layers = pl.ds(turn * depth, depth)
        for block in range(0, rows, 8):
            totals = []
            for i in range(block, block + 8):
                total = factor[0] * blurred[i, layers]
                for s in range(1, width):
                    total = total + factor[s] * blurred[i + s, layers]
                totals.append(total)
            t_high, t_low = split(jnp.concatenate(totals, axis=0))
            result = dot(jnp.concatenate([t_high, t_low], axis=1), both) + dot(t_high, low)
            predicted[turn, block : block + 8] = result.reshape(8, depth, lanes)


def gate(*rest):
    rest[-1][...] = jnp.zeros(rest[-1].shape, F32)


def turned(mine, swapped, *rest):
    received, (data, arrived) = rest[:-2], rest[-2:]
    parts, _, rows, wide = arrived.shape
    group = LANES // rows
    me = lax.axis_index("gx")
    for k in range(parts // 2):
        for core in range(2):
            source = lax.bitwise_xor(me, 2 * k + core)
            if k > 0:
                arrived[source] = received[k - 1][core]
            else:
                arrived[source] = swapped[0] if core else mine[0]
    granule = lax.broadcasted_iota(jnp.int32, (8, LANES), 1) // rows
    for slot in range(2):
        for part in range(0, parts, group):
            for eight in range(0, rows, 8):
                for piece in range(wide // LANES):
                    held = [
                        arrived[part + s, slot, eight : eight + 8, piece * LANES : (piece + 1) * LANES]
                        for s in range(group)
                    ]
                    step = 1
                    while step < group:
                        upper = (granule // step) % 2 == 1
                        crossed = list(held)
                        for s in range(group):
                            if s & step == 0:
                                one, two = held[s], held[s + step]
                                crossed[s] = jnp.where(upper, pltpu.roll(two, step * rows, 1), one)
                                crossed[s + step] = jnp.where(upper, two, pltpu.roll(one, LANES - step * rows, 1))
                        held = crossed
                        step *= 2
                    for s in range(group):
                        data[slot, eight : eight + 8, piece * group + s, part * rows : part * rows + LANES] = held[s]


def lane_blur(recorded, predicted, back):
    high, low = back[0], back[1]
    ratio = jnp.concatenate([r / p for r, p in zip(recorded, predicted)], axis=0)
    r_high, r_low = split(ratio)
    both = jnp.concatenate([high, high], axis=0)
    result = dot(jnp.concatenate([r_high, r_low], axis=1), both) + dot(r_high, low)
    return result.reshape(len(recorded), -1, result.shape[1])


def depth_blur(back, parts):
    high, low = back[0], back[1]
    s_high, s_low = split(jnp.concatenate(parts, axis=0))
    both = jnp.concatenate([high, low], axis=1)
    return dot(both, jnp.concatenate([s_high, s_high], axis=0)) + dot(high, s_low)


def spread_row(e, factor, places, backed):
    total = None
    for i, place in places.items():
        if 0 <= e - i < len(factor):
            term = factor[e - i] * backed[place]
            total = term if total is None else total + term
    return jnp.zeros(backed.shape[1:], F32) if total is None else total


def project_sides(turns, row_taps, column_taps, predicted, lane_back, depth_back, kept, outer, data, even_pair, odd_pair, backed):
    _, rows, depth, lanes = predicted.shape
    side, deep, _ = even_pair.shape
    row_list = [*range(side), *range(rows - side, rows)]
    for turn in range(VIEWS):
        if turn == 0:
            recorded = [kept[:, i] for i in row_list]
        elif turn == 2:
            recorded = [outer[:, 2 * side - 1 - j] for j in range(2 * side)]
        else:
            recorded = [data[turn // 2, rows - 1 - i if turn == 1 else i] for i in row_list]
        backed[turn] = lane_blur(recorded, [predicted[turn, i] for i in row_list], lane_back.at[turn])
    factors = [
        row_taps_of(turn, view_of(turns, turn), row_taps, column_taps, 2 * side + 1) for turn in range(VIEWS)
    ]
    places = {i: j for j, i in enumerate(row_list)}
    results = [
        depth_blur(depth_back, [spread_row(e, factors[turn], places, backed.at[turn]) for turn in range(VIEWS)])[:deep]
        for e in [*range(side), *range(rows + side, rows + 2 * side)]
    ]
    odd = is_odd("gx")
    for i in range(side):
        first, last = results[i], results[side + i]
        even_pair[i] = jnp.where(odd, first, last)
        odd_pair[i] = jnp.where(odd, last, first)


def project(turns, row_taps, column_taps, predicted, lane_back, depth_back, kept, data, outer_backed, middle, backed):
    _, rows, depth, lanes = predicted.shape
    deep = middle.shape[1]
    side = outer_backed.shape[1] // 2
    row_list = [*range(side), *range(rows - side, rows)]
    for turn in range(VIEWS):
        for j, i in enumerate(row_list):
            backed[turn, i] = outer_backed[turn, j]
        if turn == 2:
            continue
        inner = range(side, rows - side)
        if turn == 0:
            recorded = [kept[:, i] for i in inner]
        else:
            recorded = [data[turn // 2, rows - 1 - i if turn == 1 else i] for i in inner]
        backed[turn, side : rows - side] = lane_blur(recorded, [predicted[turn, i] for i in inner], lane_back.at[turn])
    factors = [
        row_taps_of(turn, view_of(turns, turn), row_taps, column_taps, 2 * side + 1) for turn in range(VIEWS)
    ]
    every, half = {i: i for i in range(rows)}, {i: i for i in row_list}
    for e in range(rows):
        parts = [
            spread_row(e + side, factors[turn], half if turn == 2 else every, backed.at[turn]) for turn in range(VIEWS)
        ]
        middle[e] = depth_blur(depth_back, parts)[:deep]


def project_half(turns, row_taps, column_taps, predicted, lane_back, half_back, flat, partial, middle, backed, inner):
    _, rows, depth, lanes = predicted.shape
    deep = middle.shape[1]
    side = (rows - inner.shape[1]) // 2
    inner[...] = flat[: depth * inner.shape[1]].reshape(inner.shape)
    row_list = range(side, rows - side)
    recorded = [inner[:, rows - side - 1 - i] for i in row_list]
    backed[side : rows - side] = lane_blur(recorded, [predicted[2, i] for i in row_list], lane_back.at[2])
    factor = row_taps_of(2, view_of(turns, 2), row_taps, column_taps, 2 * side + 1)
    back = half_back[...]
    for e in range(rows):
        s_high, s_low = split(spread_row(e + side, factor, {i: i for i in row_list}, backed))
        result = dot(back, jnp.concatenate([s_high, s_high, s_low], axis=0))
        middle[e] = partial[e] + result[:deep]


def gather_sides(middle, even_x, odd_x, own, even_pair, odd_pair):
    rows = middle.shape[0]
    side = even_x.shape[0]
    depth = own.shape[1]
    reach = even_pair.shape[0] // rows
    flip_x, flip_y = is_odd("gx"), is_odd("gy")
    for i in range(rows):
        value = middle[i]
        if i < side:
            value = value + jnp.where(flip_x, even_x[i], odd_x[i])
        if i >= rows - side:
            j = i - rows + side
            value = value + jnp.where(flip_x, odd_x[j], even_x[j])
        own[i] = value[:depth]
        before, after = value[depth : depth + reach], value[depth + reach : depth + 2 * reach]
        even_pair[i * reach : (i + 1) * reach] = jnp.where(flip_y, before, after)
        odd_pair[i * reach : (i + 1) * reach] = jnp.where(flip_y, after, before)


def finish(estimate, own, even_y, odd_y, out):
    rows, depth, lanes = own.shape
    reach = even_y.shape[0] // rows
    flip_y = is_odd("gy")
    rest = jnp.zeros((depth - reach, lanes), F32)
    for i in range(rows):
        even, odd = even_y[i * reach : (i + 1) * reach], odd_y[i * reach : (i + 1) * reach]
        first, last = jnp.where(flip_y, even, odd), jnp.where(flip_y, odd, even)
        value = own[i] + jnp.concatenate([first, rest], axis=0) + jnp.concatenate([rest, last], axis=0)
        out[:, i] = estimate[:, i] * value * (1.0 / VIEWS)


def call(body, out_shape, specs, scratch=()):
    return pl.pallas_call(
        body,
        out_shape=out_shape,
        in_specs=specs,
        out_specs=jax.tree.map(lambda _: VMEM, out_shape),
        scratch_shapes=scratch,
        compiler_params=PARAMS,
        cost_estimate=COST,
    )


def shards(estimate, recorded, quarter_turns, offsets, depth_taps, row_taps, column_taps):
    depth, rows, lanes = estimate.shape
    reach = (depth_taps.shape[1] - 1) // 2
    side = (row_taps.shape[1] - 1) // 2
    deep = depth + 2 * reach
    padded = -(-deep // 16) * 16
    parts = lax.axis_size("gx")
    even_y, odd_y = pairs(lax.axis_size("gy"))
    even_x, odd_x = pairs(parts)

    wide, chips = depth * rows, parts // 2
    edge, second = call(edges, (struct(side, depth, lanes),) * 2, [VMEM])(estimate)
    first, second = lax.ppermute(edge, "gx", even_x), lax.ppermute(second, "gx", odd_x)
    kept, mine, theirs = call(
        prepare,
        (struct(depth, rows, lanes),) + (struct(chips, 2, rows, wide),) * 2,
        [SMEM, SMEM, VMEM, ORDER],
        [pltpu.VMEM((lanes, wide), F32)],
    )(quarter_turns, offsets, recorded, first)
    mirror = [(i, parts - 1 - i) for i in range(parts)]
    swapped = lax.ppermute(theirs, "gx", [(i, i ^ 1) for i in range(parts)])
    messages = call(merge, (struct(2, 2, rows, wide),) * (chips - 1), [VMEM] * 2)(mine, swapped)
    depth_forth, lane_forth, depth_back, lane_back, half_back = call(
        matrices,
        (
            struct(VIEWS * depth, 3 * padded, dtype=BF16),
            struct(VIEWS, 2, lanes, lanes, dtype=BF16),
            struct(2, padded, VIEWS * depth, dtype=BF16),
            struct(VIEWS, 2, lanes, lanes, dtype=BF16),
            struct(padded, 3 * depth, dtype=BF16),
        ),
        [SMEM] * 5,
    )(quarter_turns, offsets, depth_taps, row_taps, column_taps)
    outer, inner = pl.pallas_call(
        pick,
        out_shape=(struct(depth, 2 * side, lanes), struct(depth, rows - 2 * side, lanes)),
        grid_spec=pltpu.PrefetchScalarGridSpec(
            num_scalar_prefetch=1,
            grid=(1,),
            in_specs=[
                pl.BlockSpec((1, depth, rows, lanes), lambda i, turns: (view_of(turns, 2), 0, 0, 0)),
                ORDER,
                ORDER,
            ],
            out_specs=[
                pl.BlockSpec((depth, 2 * side, lanes), lambda i, turns: (0, 0, 0)),
                pl.BlockSpec((depth, rows - 2 * side, lanes), lambda i, turns: (0, 0, 0)),
            ],
        ),
        compiler_params=PARAMS,
        cost_estimate=COST,
    )(quarter_turns, recorded, messages[0], half_back)
    outer = lax.ppermute(outer, "gx", mirror)
    third, fourth = call(layers_out, (struct((rows + 2 * side) * reach, lanes),) * 2, [VMEM] * 3)(estimate, first, second)
    third, fourth = lax.ppermute(third, "gy", even_y), lax.ppermute(fourth, "gy", odd_y)
    moved = {
        k: lax.ppermute(messages[k - 1], "gx", [(i, i ^ (2 * k)) for i in range(parts)])
        for k in range(chips - 1, 0, -1)
    }

    arrivals = list(moved.values())
    passed = call(gate, struct(8, LANES), [ORDER] * len(arrivals))(*arrivals)
    data = call(
        turned,
        struct(2, rows, depth, lanes),
        [VMEM] * (1 + chips),
        [pltpu.VMEM((parts, 2, rows, wide), F32)],
    )(mine, swapped, *[moved[k] for k in range(1, chips)])

    predicted = call(
        predict,
        struct(VIEWS, rows, depth, lanes),
        [SMEM] * 3 + [VMEM] * 7 + [ORDER],
        [
            pltpu.VMEM((rows + 2 * side, padded, lanes), F32),
            pltpu.VMEM((rows + 2 * side, VIEWS * depth, lanes), F32),
        ],
    )(quarter_turns, row_taps, column_taps, depth_forth, lane_forth, estimate, first, second, third, fourth, passed)

    inner = call(hold, struct(side * deep + 8, lanes), [VMEM] + [ORDER] * 2)(inner, predicted, outer)
    inner = lax.ppermute(inner, "gx", mirror)
    first, second, backed = call(
        project_sides,
        (struct(side, deep, lanes),) * 2 + (struct(VIEWS, 2 * side, depth, lanes),),
        [SMEM] * 3 + [VMEM] * 6,
    )(quarter_turns, row_taps, column_taps, predicted, lane_back, depth_back, kept, outer, data)
    first, second = lax.ppermute(first, "gx", even_x), lax.ppermute(second, "gx", odd_x)
    middle = call(
        project,
        struct(rows, deep, lanes),
        [SMEM] * 3 + [VMEM] * 6,
        [pltpu.VMEM((VIEWS, rows, depth, lanes), F32)],
    )(quarter_turns, row_taps, column_taps, predicted, lane_back, depth_back, kept, data, backed)
    middle = call(
        project_half,
        struct(rows, deep, lanes),
        [SMEM] * 3 + [VMEM] * 5,
        [pltpu.VMEM((rows, depth, lanes), F32), pltpu.VMEM((depth, rows - 2 * side, lanes), F32)],
    )(quarter_turns, row_taps, column_taps, predicted, lane_back, half_back, inner, middle)
    own, third, fourth = call(
        gather_sides,
        (struct(rows, depth, lanes), struct(rows * reach, lanes), struct(rows * reach, lanes)),
        [VMEM] * 3,
    )(middle, first, second)
    third, fourth = lax.ppermute(third, "gy", even_y), lax.ppermute(fourth, "gy", odd_y)
    return call(finish, struct(depth, rows, lanes), [VMEM] * 4)(estimate, own, third, fourth)


def solution(mesh):
    in_specs = (P("gy", "gx", None), P(None, "gy", "gx", None), P(), P(), P(), P(), P())
    out_specs = P("gy", "gx", None)
    return jax.shard_map(shards, mesh=mesh, in_specs=in_specs, out_specs=out_specs, check_vma=False)
```

```python
import functools

import jax
import jax.numpy as jnp
from jax import lax
from jax.experimental import pallas as pl
from jax.experimental.pallas import tpu as pltpu
from jax.sharding import PartitionSpec as P

VIEWS = 4
LANES = 128
VMEM = pl.BlockSpec(memory_space=pltpu.VMEM)
ORDER = pl.BlockSpec(memory_space=pl.ANY)
SMEM = pl.BlockSpec(memory_space=pltpu.SMEM)
PARAMS = pltpu.CompilerParams(vmem_limit_bytes=24 * 1024 * 1024)
F32 = jnp.float32
BF16 = jnp.bfloat16
COST = pl.CostEstimate(flops=1, bytes_accessed=1, transcendentals=0)


def struct(*shape, dtype=F32):
    return jax.ShapeDtypeStruct(shape, dtype)


def view_of(turns_ref, turn):
    found = jnp.int32(0)
    for view in range(1, VIEWS):
        found = jnp.where(turns_ref[view] == turn, jnp.int32(view), found)
    return found


def split(value):
    high = value.astype(BF16)
    return high, (value - high.astype(F32)).astype(BF16)


def dot(left, right):
    return jnp.dot(left, right, preferred_element_type=F32)


def pairs(width):
    def swaps(initial):
        return [p for i in range(initial, width - 1, 2) for p in ((i, i + 1), (i + 1, i))]

    return swaps(0), swaps(1)


def is_odd(axis):
    return lax.rem(lax.axis_index(axis), 2) == 1


def pick(turns, recorded, later, later_too, outer, inner):
    rows = recorded.shape[2]
    half = outer.shape[1] // 2
    outer[:, :half] = recorded[0, :, :half]
    outer[:, half:] = recorded[0, :, rows - half :]
    inner[...] = recorded[0, :, half : rows - half]


def prepare(turns, offsets, recorded, later, kept, mine, theirs, across):
    depth, rows, lanes = recorded.shape[1:]
    chips, _, _, wide = mine.shape
    me = lax.axis_index("gx")
    kept[...] = recorded[view_of(turns, 0)]
    for slot, turn in enumerate((1, 3)):
        view = view_of(turns, turn)
        volume = recorded[view].reshape(depth * rows, lanes)
        volume = pltpu.roll(volume, lax.rem(lanes - offsets[view], lanes), 1)
        across[...] = volume.T
        for k in range(2 * chips):
            to = lax.bitwise_xor(me, k)
            part = 2 * chips - 1 - to if turn == 1 else to
            block = across[pl.ds(pl.multiple_of(part * rows, rows), rows)]
            if k % 2 == 0:
                mine[k // 2, slot] = block
            else:
                theirs[k // 2, slot] = block


def merge(mine, swapped, *outs):
    for k in range(1, mine.shape[0]):
        for slot in range(2):
            outs[k - 1][0, slot] = mine[k, slot]
            outs[k - 1][1, slot] = swapped[k, slot]


def hold(inner, *rest):
    flat = rest[-1]
    depth, count, lanes = inner.shape
    flat[: depth * count] = inner[...].reshape(depth * count, lanes)
    flat[depth * count :] = jnp.zeros((flat.shape[0] - depth * count, lanes), F32)


def edges(own, even_pair, odd_pair):
    rows = own.shape[1]
    side = even_pair.shape[0]
    odd = is_odd("gx")
    for i in range(side):
        first, last = own[:, i], own[:, rows - side + i]
        even_pair[i] = jnp.where(odd, first, last)
        odd_pair[i] = jnp.where(odd, last, first)


def layers_out(own, from_even, from_odd, even_pair, odd_pair):
    depth, rows, _ = own.shape
    side = from_even.shape[0]
    reach = even_pair.shape[0] // (rows + 2 * side)
    odd_x, odd_y = is_odd("gx"), is_odd("gy")
    for e in range(rows + 2 * side):
        if e < side:
            value = jnp.where(odd_x, from_even[e], from_odd[e])
        elif e < side + rows:
            value = own[:, e - side]
        else:
            value = jnp.where(odd_x, from_odd[e - side - rows], from_even[e - side - rows])
        first, last = value[:reach], value[depth - reach :]
        even_pair[e * reach : (e + 1) * reach] = jnp.where(odd_y, first, last)
        odd_pair[e * reach : (e + 1) * reach] = jnp.where(odd_y, last, first)


def row_taps_of(turn, view, row_taps, column_taps, width):
    source = column_taps if turn % 2 else row_taps
    flipped = turn in (1, 2)
    return [source[view, width - 1 - s if flipped else s] for s in range(width)]


def matrices(turns, offsets, depth_taps, row_taps, column_taps, depth_forth, lane_forth, depth_back, lane_back, half_back):
    padded = depth_back.shape[1]
    depth = half_back.shape[1] // 3
    lanes = lane_back.shape[2]
    reach = (depth_taps.shape[1] - 1) // 2
    width = row_taps.shape[1]
    deep = depth + 2 * reach
    views = [view_of(turns, turn) for turn in range(VIEWS)]
    column = lax.broadcasted_iota(jnp.int32, (depth, LANES), 1)
    row = lax.broadcasted_iota(jnp.int32, (depth, LANES), 0)
    layer = jnp.where(column < depth, column, jnp.where(column < depth + reach, column - depth - reach, column - reach))
    tap = jnp.where(column < deep, layer - row + reach, -1)
    stacked = []
    for view in views:
        matrix = jnp.zeros((depth, LANES), F32)
        for t in range(2 * reach + 1):
            matrix = jnp.where(tap == t, depth_taps[view, t], matrix)
        stacked.append(matrix)
    matrix = jnp.concatenate(stacked, axis=0)
    back_high, back_low = split(matrix.T[:padded])
    depth_back[0] = back_high
    depth_back[1] = back_low
    half = slice(2 * depth, 3 * depth)
    half_back[...] = jnp.concatenate([back_high[:, half], back_low[:, half], back_high[:, half]], axis=1)
    high, low = split(matrix)
    depth_forth[...] = jnp.concatenate([high[:, :padded], low[:, :padded], high[:, :padded]], axis=1)
    inward = lax.broadcasted_iota(jnp.int32, (lanes, lanes), 0)
    outward = lax.broadcasted_iota(jnp.int32, (lanes, lanes), 1)
    for turn, view in enumerate(views):
        place = outward
        if turn % 2 == 0:
            place = outward - offsets[view]
            place = jnp.where(place < 0, place + lanes, place)
        tap = (lanes - 1 - place - inward if turn >= 2 else inward - place) + width // 2
        source = row_taps if turn % 2 else column_taps
        matrix = jnp.zeros((lanes, lanes), F32)
        for r in range(width):
            matrix = jnp.where(tap == r, source[view, r], matrix)
        high, low = split(matrix)
        lane_forth[turn, 0] = high
        lane_forth[turn, 1] = low
        back_high, back_low = split(matrix.T)
        lane_back[turn, 0] = back_high
        lane_back[turn, 1] = back_low


def predict(turns, row_taps, column_taps, depth_forth, lane_forth, own, even_x, odd_x, even_y, odd_y, later,
            predicted, extended, blurred):
    depth, rows, lanes = own.shape
    side = even_x.shape[0]
    reach = even_y.shape[0] // (rows + 2 * side)
    width = 2 * side + 1
    deep = depth + 2 * reach
    padded = extended.shape[1]
    forth = depth_forth[...]

    flip_x, flip_y = is_odd("gx"), is_odd("gy")
    for e in range(rows + 2 * side):
        if e < side:
            extended[e, 0:depth] = jnp.where(flip_x, even_x[e], odd_x[e])
        elif e < side + rows:
            extended[e, 0:depth] = own[:, e - side]
        else:
            extended[e, 0:depth] = jnp.where(flip_x, odd_x[e - side - rows], even_x[e - side - rows])
        even, odd = even_y[e * reach : (e + 1) * reach], odd_y[e * reach : (e + 1) * reach]
        extended[e, depth : depth + reach] = jnp.where(flip_y, even, odd)
        extended[e, depth + reach : deep] = jnp.where(flip_y, odd, even)
        if padded > deep:
            extended[e, deep:padded] = jnp.zeros((padded - deep, lanes), F32)

    for i in range(0, rows + 2 * side, 2):
        e_high, e_low = split(jnp.concatenate([extended[i], extended[i + 1]], axis=1))
        result = dot(forth, jnp.concatenate([e_high, e_high, e_low], axis=0))
        blurred[i] = result[:, :lanes]
        blurred[i + 1] = result[:, lanes:]

    for turn in range(VIEWS):
        view = view_of(turns, turn)
        high, low = lane_forth[turn, 0], lane_forth[turn, 1]
        both = jnp.concatenate([high, high], axis=0)
        factor = row_taps_of(turn, view, row_taps, column_taps, width)
        layers = pl.ds(turn * depth, depth)
        for block in range(0, rows, 8):
            totals = []
            for i in range(block, block + 8):
                total = factor[0] * blurred[i, layers]
                for s in range(1, width):
                    total = total + factor[s] * blurred[i + s, layers]
                totals.append(total)
            t_high, t_low = split(jnp.concatenate(totals, axis=0))
            result = dot(jnp.concatenate([t_high, t_low], axis=1), both) + dot(t_high, low)
            predicted[turn, block : block + 8] = result.reshape(8, depth, lanes)


def gate(*rest):
    rest[-1][...] = jnp.zeros(rest[-1].shape, F32)


def turned(mine, swapped, *rest):
    received, (data, arrived) = rest[:-2], rest[-2:]
    parts, _, rows, wide = arrived.shape
    group = LANES // rows
    me = lax.axis_index("gx")
    for k in range(parts // 2):
        for core in range(2):
            source = lax.bitwise_xor(me, 2 * k + core)
            if k > 0:
                arrived[source] = received[k - 1][core]
            else:
                arrived[source] = swapped[0] if core else mine[0]
    granule = lax.broadcasted_iota(jnp.int32, (8, LANES), 1) // rows
    for slot in range(2):
        for part in range(0, parts, group):
            for eight in range(0, rows, 8):
                for piece in range(wide // LANES):
                    held = [
                        arrived[part + s, slot, eight : eight + 8, piece * LANES : (piece + 1) * LANES]
                        for s in range(group)
                    ]
                    step = 1
                    while step < group:
                        upper = (granule // step) % 2 == 1
                        crossed = list(held)
                        for s in range(group):
                            if s & step == 0:
                                one, two = held[s], held[s + step]
                                crossed[s] = jnp.where(upper, pltpu.roll(two, step * rows, 1), one)
                                crossed[s + step] = jnp.where(upper, two, pltpu.roll(one, LANES - step * rows, 1))
                        held = crossed
                        step *= 2
                    for s in range(group):
                        data[slot, eight : eight + 8, piece * group + s, part * rows : part * rows + LANES] = held[s]


def lane_blur(recorded, predicted, back):
    high, low = back[0], back[1]
    ratio = jnp.concatenate([r / p for r, p in zip(recorded, predicted)], axis=0)
    r_high, r_low = split(ratio)
    both = jnp.concatenate([high, high], axis=0)
    result = dot(jnp.concatenate([r_high, r_low], axis=1), both) + dot(r_high, low)
    return result.reshape(len(recorded), -1, result.shape[1])


def depth_blur(back, parts):
    high, low = back[0], back[1]
    s_high, s_low = split(jnp.concatenate(parts, axis=0))
    both = jnp.concatenate([high, low], axis=1)
    return dot(both, jnp.concatenate([s_high, s_high], axis=0)) + dot(high, s_low)


def spread_row(e, factor, places, backed):
    total = None
    for i, place in places.items():
        if 0 <= e - i < len(factor):
            term = factor[e - i] * backed[place]
            total = term if total is None else total + term
    return jnp.zeros(backed.shape[1:], F32) if total is None else total


def project_sides(turns, row_taps, column_taps, predicted, lane_back, depth_back, kept, outer, data, even_pair, odd_pair, backed):
    _, rows, depth, lanes = predicted.shape
    side, deep, _ = even_pair.shape
    row_list = [*range(side), *range(rows - side, rows)]
    for turn in range(VIEWS):
        if turn == 0:
            recorded = [kept[:, i] for i in row_list]
        elif turn == 2:
            recorded = [outer[:, 2 * side - 1 - j] for j in range(2 * side)]
        else:
            recorded = [data[turn // 2, rows - 1 - i if turn == 1 else i] for i in row_list]
        backed[turn] = lane_blur(recorded, [predicted[turn, i] for i in row_list], lane_back.at[turn])
    factors = [
        row_taps_of(turn, view_of(turns, turn), row_taps, column_taps, 2 * side + 1) for turn in range(VIEWS)
    ]
    places = {i: j for j, i in enumerate(row_list)}
    results = [
        depth_blur(depth_back, [spread_row(e, factors[turn], places, backed.at[turn]) for turn in range(VIEWS)])[:deep]
        for e in [*range(side), *range(rows + side, rows + 2 * side)]
    ]
    odd = is_odd("gx")
    for i in range(side):
        first, last = results[i], results[side + i]
        even_pair[i] = jnp.where(odd, first, last)
        odd_pair[i] = jnp.where(odd, last, first)


def project(turns, row_taps, column_taps, predicted, lane_back, depth_back, kept, data, outer_backed, middle, backed):
    _, rows, depth, lanes = predicted.shape
    deep = middle.shape[1]
    side = outer_backed.shape[1] // 2
    row_list = [*range(side), *range(rows - side, rows)]
    for turn in range(VIEWS):
        for j, i in enumerate(row_list):
            backed[turn, i] = outer_backed[turn, j]
        if turn == 2:
            continue
        inner = range(side, rows - side)
        if turn == 0:
            recorded = [kept[:, i] for i in inner]
        else:
            recorded = [data[turn // 2, rows - 1 - i if turn == 1 else i] for i in inner]
        backed[turn, side : rows - side] = lane_blur(recorded, [predicted[turn, i] for i in inner], lane_back.at[turn])
    factors = [
        row_taps_of(turn, view_of(turns, turn), row_taps, column_taps, 2 * side + 1) for turn in range(VIEWS)
    ]
    every, half = {i: i for i in range(rows)}, {i: i for i in row_list}
    for e in range(rows):
        parts = [
            spread_row(e + side, factors[turn], half if turn == 2 else every, backed.at[turn]) for turn in range(VIEWS)
        ]
        middle[e] = depth_blur(depth_back, parts)[:deep]


def project_half(turns, row_taps, column_taps, predicted, lane_back, half_back, flat, partial, middle, backed, inner):
    _, rows, depth, lanes = predicted.shape
    deep = middle.shape[1]
    side = (rows - inner.shape[1]) // 2
    inner[...] = flat[: depth * inner.shape[1]].reshape(inner.shape)
    row_list = range(side, rows - side)
    recorded = [inner[:, rows - side - 1 - i] for i in row_list]
    backed[side : rows - side] = lane_blur(recorded, [predicted[2, i] for i in row_list], lane_back.at[2])
    factor = row_taps_of(2, view_of(turns, 2), row_taps, column_taps, 2 * side + 1)
    back = half_back[...]
    for e in range(rows):
        s_high, s_low = split(spread_row(e + side, factor, {i: i for i in row_list}, backed))
        result = dot(back, jnp.concatenate([s_high, s_high, s_low], axis=0))
        middle[e] = partial[e] + result[:deep]


def gather_sides(middle, even_x, odd_x, own, even_pair, odd_pair):
    rows = middle.shape[0]
    side = even_x.shape[0]
    depth = own.shape[1]
    reach = even_pair.shape[0] // rows
    flip_x, flip_y = is_odd("gx"), is_odd("gy")
    for i in range(rows):
        value = middle[i]
        if i < side:
            value = value + jnp.where(flip_x, even_x[i], odd_x[i])
        if i >= rows - side:
            j = i - rows + side
            value = value + jnp.where(flip_x, odd_x[j], even_x[j])
        own[i] = value[:depth]
        before, after = value[depth : depth + reach], value[depth + reach : depth + 2 * reach]
        even_pair[i * reach : (i + 1) * reach] = jnp.where(flip_y, before, after)
        odd_pair[i * reach : (i + 1) * reach] = jnp.where(flip_y, after, before)


def finish(estimate, own, even_y, odd_y, out):
    rows, depth, lanes = own.shape
    reach = even_y.shape[0] // rows
    flip_y = is_odd("gy")
    rest = jnp.zeros((depth - reach, lanes), F32)
    for i in range(rows):
        even, odd = even_y[i * reach : (i + 1) * reach], odd_y[i * reach : (i + 1) * reach]
        first, last = jnp.where(flip_y, even, odd), jnp.where(flip_y, odd, even)
        value = own[i] + jnp.concatenate([first, rest], axis=0) + jnp.concatenate([rest, last], axis=0)
        out[:, i] = estimate[:, i] * value * (1.0 / VIEWS)


def call(body, out_shape, specs, scratch=()):
    return pl.pallas_call(
        body,
        out_shape=out_shape,
        in_specs=specs,
        out_specs=jax.tree.map(lambda _: VMEM, out_shape),
        scratch_shapes=scratch,
        compiler_params=PARAMS,
        cost_estimate=COST,
    )


def shards(estimate, recorded, quarter_turns, offsets, depth_taps, row_taps, column_taps):
    depth, rows, lanes = estimate.shape
    reach = (depth_taps.shape[1] - 1) // 2
    side = (row_taps.shape[1] - 1) // 2
    deep = depth + 2 * reach
    padded = -(-deep // 16) * 16
    parts = lax.axis_size("gx")
    even_y, odd_y = pairs(lax.axis_size("gy"))
    even_x, odd_x = pairs(parts)

    wide, chips = depth * rows, parts // 2
    edge, second = call(edges, (struct(side, depth, lanes),) * 2, [VMEM])(estimate)
    first, second = lax.ppermute(edge, "gx", even_x), lax.ppermute(second, "gx", odd_x)
    kept, mine, theirs = call(
        prepare,
        (struct(depth, rows, lanes),) + (struct(chips, 2, rows, wide),) * 2,
        [SMEM, SMEM, VMEM, ORDER],
        [pltpu.VMEM((lanes, wide), F32)],
    )(quarter_turns, offsets, recorded, edge)
    mirror = [(i, parts - 1 - i) for i in range(parts)]
    swapped = lax.ppermute(theirs, "gx", [(i, i ^ 1) for i in range(parts)])
    messages = call(merge, (struct(2, 2, rows, wide),) * (chips - 1), [VMEM] * 2)(mine, swapped)
    depth_forth, lane_forth, depth_back, lane_back, half_back = call(
        matrices,
        (
            struct(VIEWS * depth, 3 * padded, dtype=BF16),
            struct(VIEWS, 2, lanes, lanes, dtype=BF16),
            struct(2, padded, VIEWS * depth, dtype=BF16),
            struct(VIEWS, 2, lanes, lanes, dtype=BF16),
            struct(padded, 3 * depth, dtype=BF16),
        ),
        [SMEM] * 5,
    )(quarter_turns, offsets, depth_taps, row_taps, column_taps)
    outer, inner = pl.pallas_call(
        pick,
        out_shape=(struct(depth, 2 * side, lanes), struct(depth, rows - 2 * side, lanes)),
        grid_spec=pltpu.PrefetchScalarGridSpec(
            num_scalar_prefetch=1,
            grid=(1,),
            in_specs=[
                pl.BlockSpec((1, depth, rows, lanes), lambda i, turns: (view_of(turns, 2), 0, 0, 0)),
                ORDER,
                ORDER,
            ],
            out_specs=[
                pl.BlockSpec((depth, 2 * side, lanes), lambda i, turns: (0, 0, 0)),
                pl.BlockSpec((depth, rows - 2 * side, lanes), lambda i, turns: (0, 0, 0)),
            ],
        ),
        compiler_params=PARAMS,
        cost_estimate=COST,
    )(quarter_turns, recorded, messages[0], half_back)
    outer = lax.ppermute(outer, "gx", mirror)
    third, fourth = call(layers_out, (struct((rows + 2 * side) * reach, lanes),) * 2, [VMEM] * 3)(estimate, first, second)
    third, fourth = lax.ppermute(third, "gy", even_y), lax.ppermute(fourth, "gy", odd_y)
    moved = {
        k: lax.ppermute(messages[k - 1], "gx", [(i, i ^ (2 * k)) for i in range(parts)])
        for k in range(chips - 1, 0, -1)
    }

    arrivals = list(moved.values())
    passed = call(gate, struct(8, LANES), [ORDER] * len(arrivals))(*arrivals)
    data = call(
        turned,
        struct(2, rows, depth, lanes),
        [VMEM] * (1 + chips),
        [pltpu.VMEM((parts, 2, rows, wide), F32)],
    )(mine, swapped, *[moved[k] for k in range(1, chips)])

    predicted = call(
        predict,
        struct(VIEWS, rows, depth, lanes),
        [SMEM] * 3 + [VMEM] * 7 + [ORDER],
        [
            pltpu.VMEM((rows + 2 * side, padded, lanes), F32),
            pltpu.VMEM((rows + 2 * side, VIEWS * depth, lanes), F32),
        ],
    )(quarter_turns, row_taps, column_taps, depth_forth, lane_forth, estimate, first, second, third, fourth, passed)

    inner = call(hold, struct(side * deep + 8, lanes), [VMEM] + [ORDER] * 2)(inner, predicted, outer)
    inner = lax.ppermute(inner, "gx", mirror)
    first, second, backed = call(
        project_sides,
        (struct(side, deep, lanes),) * 2 + (struct(VIEWS, 2 * side, depth, lanes),),
        [SMEM] * 3 + [VMEM] * 6,
    )(quarter_turns, row_taps, column_taps, predicted, lane_back, depth_back, kept, outer, data)
    first, second = lax.ppermute(first, "gx", even_x), lax.ppermute(second, "gx", odd_x)
    middle = call(
        project,
        struct(rows, deep, lanes),
        [SMEM] * 3 + [VMEM] * 6,
        [pltpu.VMEM((VIEWS, rows, depth, lanes), F32)],
    )(quarter_turns, row_taps, column_taps, predicted, lane_back, depth_back, kept, data, backed)
    middle = call(
        project_half,
        struct(rows, deep, lanes),
        [SMEM] * 3 + [VMEM] * 5,
        [pltpu.VMEM((rows, depth, lanes), F32), pltpu.VMEM((depth, rows - 2 * side, lanes), F32)],
    )(quarter_turns, row_taps, column_taps, predicted, lane_back, half_back, inner, middle)
    own, third, fourth = call(
        gather_sides,
        (struct(rows, depth, lanes), struct(rows * reach, lanes), struct(rows * reach, lanes)),
        [VMEM] * 3,
    )(middle, first, second)
    third, fourth = lax.ppermute(third, "gy", even_y), lax.ppermute(fourth, "gy", odd_y)
    return call(finish, struct(depth, rows, lanes), [VMEM] * 4)(estimate, own, third, fourth)


def solution(mesh):
    in_specs = (P("gy", "gx", None), P(None, "gy", "gx", None), P(), P(), P(), P(), P())
    out_specs = P("gy", "gx", None)
    return jax.shard_map(shards, mesh=mesh, in_specs=in_specs, out_specs=out_specs, check_vma=False)
```

```python
import functools

import jax
import jax.numpy as jnp
from jax import lax
from jax.experimental import pallas as pl
from jax.experimental.pallas import tpu as pltpu
from jax.sharding import PartitionSpec as P

VIEWS = 4
LANES = 128
VMEM = pl.BlockSpec(memory_space=pltpu.VMEM)
ORDER = pl.BlockSpec(memory_space=pl.ANY)
SMEM = pl.BlockSpec(memory_space=pltpu.SMEM)
PARAMS = pltpu.CompilerParams(vmem_limit_bytes=24 * 1024 * 1024)
F32 = jnp.float32
BF16 = jnp.bfloat16
COST = pl.CostEstimate(flops=1, bytes_accessed=1, transcendentals=0)


def struct(*shape, dtype=F32):
    return jax.ShapeDtypeStruct(shape, dtype)


def view_of(turns_ref, turn):
    found = jnp.int32(0)
    for view in range(1, VIEWS):
        found = jnp.where(turns_ref[view] == turn, jnp.int32(view), found)
    return found


def split(value):
    high = value.astype(BF16)
    return high, (value - high.astype(F32)).astype(BF16)


def dot(left, right):
    return jnp.dot(left, right, preferred_element_type=F32)


def pairs(width):
    def swaps(initial):
        return [p for i in range(initial, width - 1, 2) for p in ((i, i + 1), (i + 1, i))]

    return swaps(0), swaps(1)


def is_odd(axis):
    return lax.rem(lax.axis_index(axis), 2) == 1


def pick(turns, recorded, later, outer, inner):
    rows = recorded.shape[2]
    half = outer.shape[1] // 2
    outer[:, :half] = recorded[0, :, :half]
    outer[:, half:] = recorded[0, :, rows - half :]
    inner[...] = recorded[0, :, half : rows - half]


def prepare(turns, offsets, recorded, later, kept, mine, theirs, across):
    depth, rows, lanes = recorded.shape[1:]
    chips, _, _, wide = mine.shape
    me = lax.axis_index("gx")
    kept[...] = recorded[view_of(turns, 0)]
    for slot, turn in enumerate((1, 3)):
        view = view_of(turns, turn)
        volume = recorded[view].reshape(depth * rows, lanes)
        volume = pltpu.roll(volume, lax.rem(lanes - offsets[view], lanes), 1)
        across[...] = volume.T
        for k in range(2 * chips):
            to = lax.bitwise_xor(me, k)
            part = 2 * chips - 1 - to if turn == 1 else to
            block = across[pl.ds(pl.multiple_of(part * rows, rows), rows)]
            if k % 2 == 0:
                mine[k // 2, slot] = block
            else:
                theirs[k // 2, slot] = block


def merge(mine, swapped, *outs):
    for k in range(1, mine.shape[0]):
        for slot in range(2):
            outs[k - 1][0, slot] = mine[k, slot]
            outs[k - 1][1, slot] = swapped[k, slot]


def hold(inner, *rest):
    flat = rest[-1]
    depth, count, lanes = inner.shape
    flat[: depth * count] = inner[...].reshape(depth * count, lanes)
    flat[depth * count :] = jnp.zeros((flat.shape[0] - depth * count, lanes), F32)


def edges(own, even_pair, odd_pair):
    rows = own.shape[1]
    side = even_pair.shape[0]
    odd = is_odd("gx")
    for i in range(side):
        first, last = own[:, i], own[:, rows - side + i]
        even_pair[i] = jnp.where(odd, first, last)
        odd_pair[i] = jnp.where(odd, last, first)


def layers_out(own, from_even, from_odd, even_pair, odd_pair):
    depth, rows, _ = own.shape
    side = from_even.shape[0]
    reach = even_pair.shape[0] // (rows + 2 * side)
    odd_x, odd_y = is_odd("gx"), is_odd("gy")
    for e in range(rows + 2 * side):
        if e < side:
            value = jnp.where(odd_x, from_even[e], from_odd[e])
        elif e < side + rows:
            value = own[:, e - side]
        else:
            value = jnp.where(odd_x, from_odd[e - side - rows], from_even[e - side - rows])
        first, last = value[:reach], value[depth - reach :]
        even_pair[e * reach : (e + 1) * reach] = jnp.where(odd_y, first, last)
        odd_pair[e * reach : (e + 1) * reach] = jnp.where(odd_y, last, first)


def row_taps_of(turn, view, row_taps, column_taps, width):
    source = column_taps if turn % 2 else row_taps
    flipped = turn in (1, 2)
    return [source[view, width - 1 - s if flipped else s] for s in range(width)]


def matrices(turns, offsets, depth_taps, row_taps, column_taps, depth_forth, lane_forth, depth_back, lane_back, half_back):
    padded = depth_back.shape[1]
    depth = half_back.shape[1] // 3
    lanes = lane_back.shape[2]
    reach = (depth_taps.shape[1] - 1) // 2
    width = row_taps.shape[1]
    deep = depth + 2 * reach
    views = [view_of(turns, turn) for turn in range(VIEWS)]
    column = lax.broadcasted_iota(jnp.int32, (depth, LANES), 1)
    row = lax.broadcasted_iota(jnp.int32, (depth, LANES), 0)
    layer = jnp.where(column < depth, column, jnp.where(column < depth + reach, column - depth - reach, column - reach))
    tap = jnp.where(column < deep, layer - row + reach, -1)
    stacked = []
    for view in views:
        matrix = jnp.zeros((depth, LANES), F32)
        for t in range(2 * reach + 1):
            matrix = jnp.where(tap == t, depth_taps[view, t], matrix)
        stacked.append(matrix)
    matrix = jnp.concatenate(stacked, axis=0)
    back_high, back_low = split(matrix.T[:padded])
    depth_back[0] = back_high
    depth_back[1] = back_low
    half = slice(2 * depth, 3 * depth)
    half_back[...] = jnp.concatenate([back_high[:, half], back_low[:, half], back_high[:, half]], axis=1)
    high, low = split(matrix)
    depth_forth[...] = jnp.concatenate([high[:, :padded], low[:, :padded], high[:, :padded]], axis=1)
    inward = lax.broadcasted_iota(jnp.int32, (lanes, lanes), 0)
    outward = lax.broadcasted_iota(jnp.int32, (lanes, lanes), 1)
    for turn, view in enumerate(views):
        place = outward
        if turn % 2 == 0:
            place = outward - offsets[view]
            place = jnp.where(place < 0, place + lanes, place)
        tap = (lanes - 1 - place - inward if turn >= 2 else inward - place) + width // 2
        source = row_taps if turn % 2 else column_taps
        matrix = jnp.zeros((lanes, lanes), F32)
        for r in range(width):
            matrix = jnp.where(tap == r, source[view, r], matrix)
        high, low = split(matrix)
        lane_forth[turn, 0] = high
        lane_forth[turn, 1] = low
        back_high, back_low = split(matrix.T)
        lane_back[turn, 0] = back_high
        lane_back[turn, 1] = back_low


def predict(turns, row_taps, column_taps, depth_forth, lane_forth, own, even_x, odd_x, even_y, odd_y, later,
            predicted, extended, blurred):
    depth, rows, lanes = own.shape
    side = even_x.shape[0]
    reach = even_y.shape[0] // (rows + 2 * side)
    width = 2 * side + 1
    deep = depth + 2 * reach
    padded = extended.shape[1]
    forth = depth_forth[...]

    flip_x, flip_y = is_odd("gx"), is_odd("gy")
    for e in range(rows + 2 * side):
        if e < side:
            extended[e, 0:depth] = jnp.where(flip_x, even_x[e], odd_x[e])
        elif e < side + rows:
            extended[e, 0:depth] = own[:, e - side]
        else:
            extended[e, 0:depth] = jnp.where(flip_x, odd_x[e - side - rows], even_x[e - side - rows])
        even, odd = even_y[e * reach : (e + 1) * reach], odd_y[e * reach : (e + 1) * reach]
        extended[e, depth : depth + reach] = jnp.where(flip_y, even, odd)
        extended[e, depth + reach : deep] = jnp.where(flip_y, odd, even)
        if padded > deep:
            extended[e, deep:padded] = jnp.zeros((padded - deep, lanes), F32)

    for i in range(0, rows + 2 * side, 2):
        e_high, e_low = split(jnp.concatenate([extended[i], extended[i + 1]], axis=1))
        result = dot(forth, jnp.concatenate([e_high, e_high, e_low], axis=0))
        blurred[i] = result[:, :lanes]
        blurred[i + 1] = result[:, lanes:]

    for turn in range(VIEWS):
        view = view_of(turns, turn)
        high, low = lane_forth[turn, 0], lane_forth[turn, 1]
        both = jnp.concatenate([high, high], axis=0)
        factor = row_taps_of(turn, view, row_taps, column_taps, width)
        layers = pl.ds(turn * depth, depth)
        for block in range(0, rows, 8):
            totals = []
            for i in range(block, block + 8):
                total = factor[0] * blurred[i, layers]
                for s in range(1, width):
                    total = total + factor[s] * blurred[i + s, layers]
                totals.append(total)
            t_high, t_low = split(jnp.concatenate(totals, axis=0))
            result = dot(jnp.concatenate([t_high, t_low], axis=1), both) + dot(t_high, low)
            predicted[turn, block : block + 8] = result.reshape(8, depth, lanes)


def gate(*rest):
    rest[-1][...] = jnp.zeros(rest[-1].shape, F32)


def turned(mine, swapped, *rest):
    received, (data, arrived) = rest[:-2], rest[-2:]
    parts, _, rows, wide = arrived.shape
    group = LANES // rows
    me = lax.axis_index("gx")
    for k in range(parts // 2):
        for core in range(2):
            source = lax.bitwise_xor(me, 2 * k + core)
            if k > 0:
                arrived[source] = received[k - 1][core]
            else:
                arrived[source] = swapped[0] if core else mine[0]
    granule = lax.broadcasted_iota(jnp.int32, (8, LANES), 1) // rows
    for slot in range(2):
        for part in range(0, parts, group):
            for eight in range(0, rows, 8):
                for piece in range(wide // LANES):
                    held = [
                        arrived[part + s, slot, eight : eight + 8, piece * LANES : (piece + 1) * LANES]
                        for s in range(group)
                    ]
                    step = 1
                    while step < group:
                        upper = (granule // step) % 2 == 1
                        crossed = list(held)
                        for s in range(group):
                            if s & step == 0:
                                one, two = held[s], held[s + step]
                                crossed[s] = jnp.where(upper, pltpu.roll(two, step * rows, 1), one)
                                crossed[s + step] = jnp.where(upper, two, pltpu.roll(one, LANES - step * rows, 1))
                        held = crossed
                        step *= 2
                    for s in range(group):
                        data[slot, eight : eight + 8, piece * group + s, part * rows : part * rows + LANES] = held[s]


def lane_blur(recorded, predicted, back):
    high, low = back[0], back[1]
    ratio = jnp.concatenate([r / p for r, p in zip(recorded, predicted)], axis=0)
    r_high, r_low = split(ratio)
    both = jnp.concatenate([high, high], axis=0)
    result = dot(jnp.concatenate([r_high, r_low], axis=1), both) + dot(r_high, low)
    return result.reshape(len(recorded), -1, result.shape[1])


def depth_blur(back, parts):
    high, low = back[0], back[1]
    s_high, s_low = split(jnp.concatenate(parts, axis=0))
    both = jnp.concatenate([high, low], axis=1)
    return dot(both, jnp.concatenate([s_high, s_high], axis=0)) + dot(high, s_low)


def spread_row(e, factor, places, backed):
    total = None
    for i, place in places.items():
        if 0 <= e - i < len(factor):
            term = factor[e - i] * backed[place]
            total = term if total is None else total + term
    return jnp.zeros(backed.shape[1:], F32) if total is None else total


def project_sides(turns, row_taps, column_taps, predicted, lane_back, depth_back, kept, outer, data, even_pair, odd_pair, backed):
    _, rows, depth, lanes = predicted.shape
    side, deep, _ = even_pair.shape
    row_list = [*range(side), *range(rows - side, rows)]
    for turn in range(VIEWS):
        if turn == 0:
            recorded = [kept[:, i] for i in row_list]
        elif turn == 2:
            recorded = [outer[:, 2 * side - 1 - j] for j in range(2 * side)]
        else:
            recorded = [data[turn // 2, rows - 1 - i if turn == 1 else i] for i in row_list]
        backed[turn] = lane_blur(recorded, [predicted[turn, i] for i in row_list], lane_back.at[turn])
    factors = [
        row_taps_of(turn, view_of(turns, turn), row_taps, column_taps, 2 * side + 1) for turn in range(VIEWS)
    ]
    places = {i: j for j, i in enumerate(row_list)}
    results = [
        depth_blur(depth_back, [spread_row(e, factors[turn], places, backed.at[turn]) for turn in range(VIEWS)])[:deep]
        for e in [*range(side), *range(rows + side, rows + 2 * side)]
    ]
    odd = is_odd("gx")
    for i in range(side):
        first, last = results[i], results[side + i]
        even_pair[i] = jnp.where(odd, first, last)
        odd_pair[i] = jnp.where(odd, last, first)


def project(turns, row_taps, column_taps, predicted, lane_back, depth_back, kept, data, outer_backed, middle, backed):
    _, rows, depth, lanes = predicted.shape
    deep = middle.shape[1]
    side = outer_backed.shape[1] // 2
    row_list = [*range(side), *range(rows - side, rows)]
    for turn in range(VIEWS):
        for j, i in enumerate(row_list):
            backed[turn, i] = outer_backed[turn, j]
        if turn == 2:
            continue
        inner = range(side, rows - side)
        if turn == 0:
            recorded = [kept[:, i] for i in inner]
        else:
            recorded = [data[turn // 2, rows - 1 - i if turn == 1 else i] for i in inner]
        backed[turn, side : rows - side] = lane_blur(recorded, [predicted[turn, i] for i in inner], lane_back.at[turn])
    factors = [
        row_taps_of(turn, view_of(turns, turn), row_taps, column_taps, 2 * side + 1) for turn in range(VIEWS)
    ]
    every, half = {i: i for i in range(rows)}, {i: i for i in row_list}
    for e in range(rows):
        parts = [
            spread_row(e + side, factors[turn], half if turn == 2 else every, backed.at[turn]) for turn in range(VIEWS)
        ]
        middle[e] = depth_blur(depth_back, parts)[:deep]


def project_half(turns, row_taps, column_taps, predicted, lane_back, half_back, flat, partial, middle, backed, inner):
    _, rows, depth, lanes = predicted.shape
    deep = middle.shape[1]
    side = (rows - inner.shape[1]) // 2
    inner[...] = flat[: depth * inner.shape[1]].reshape(inner.shape)
    row_list = range(side, rows - side)
    recorded = [inner[:, rows - side - 1 - i] for i in row_list]
    backed[side : rows - side] = lane_blur(recorded, [predicted[2, i] for i in row_list], lane_back.at[2])
    factor = row_taps_of(2, view_of(turns, 2), row_taps, column_taps, 2 * side + 1)
    back = half_back[...]
    for e in range(rows):
        s_high, s_low = split(spread_row(e + side, factor, {i: i for i in row_list}, backed))
        result = dot(back, jnp.concatenate([s_high, s_high, s_low], axis=0))
        middle[e] = partial[e] + result[:deep]


def gather_sides(middle, even_x, odd_x, own, even_pair, odd_pair):
    rows = middle.shape[0]
    side = even_x.shape[0]
    depth = own.shape[1]
    reach = even_pair.shape[0] // rows
    flip_x, flip_y = is_odd("gx"), is_odd("gy")
    for i in range(rows):
        value = middle[i]
        if i < side:
            value = value + jnp.where(flip_x, even_x[i], odd_x[i])
        if i >= rows - side:
            j = i - rows + side
            value = value + jnp.where(flip_x, odd_x[j], even_x[j])
        own[i] = value[:depth]
        before, after = value[depth : depth + reach], value[depth + reach : depth + 2 * reach]
        even_pair[i * reach : (i + 1) * reach] = jnp.where(flip_y, before, after)
        odd_pair[i * reach : (i + 1) * reach] = jnp.where(flip_y, after, before)


def finish(estimate, own, even_y, odd_y, out):
    rows, depth, lanes = own.shape
    reach = even_y.shape[0] // rows
    flip_y = is_odd("gy")
    rest = jnp.zeros((depth - reach, lanes), F32)
    for i in range(rows):
        even, odd = even_y[i * reach : (i + 1) * reach], odd_y[i * reach : (i + 1) * reach]
        first, last = jnp.where(flip_y, even, odd), jnp.where(flip_y, odd, even)
        value = own[i] + jnp.concatenate([first, rest], axis=0) + jnp.concatenate([rest, last], axis=0)
        out[:, i] = estimate[:, i] * value * (1.0 / VIEWS)


def call(body, out_shape, specs, scratch=()):
    return pl.pallas_call(
        body,
        out_shape=out_shape,
        in_specs=specs,
        out_specs=jax.tree.map(lambda _: VMEM, out_shape),
        scratch_shapes=scratch,
        compiler_params=PARAMS,
        cost_estimate=COST,
    )


def shards(estimate, recorded, quarter_turns, offsets, depth_taps, row_taps, column_taps):
    depth, rows, lanes = estimate.shape
    reach = (depth_taps.shape[1] - 1) // 2
    side = (row_taps.shape[1] - 1) // 2
    deep = depth + 2 * reach
    padded = -(-deep // 16) * 16
    parts = lax.axis_size("gx")
    even_y, odd_y = pairs(lax.axis_size("gy"))
    even_x, odd_x = pairs(parts)

    wide, chips = depth * rows, parts // 2
    edge, second = call(edges, (struct(side, depth, lanes),) * 2, [VMEM])(estimate)
    first, second = lax.ppermute(edge, "gx", even_x), lax.ppermute(second, "gx", odd_x)
    kept, mine, theirs = call(
        prepare,
        (struct(depth, rows, lanes),) + (struct(chips, 2, rows, wide),) * 2,
        [SMEM, SMEM, VMEM, ORDER],
        [pltpu.VMEM((lanes, wide), F32)],
    )(quarter_turns, offsets, recorded, edge)
    mirror = [(i, parts - 1 - i) for i in range(parts)]
    swapped = lax.ppermute(theirs, "gx", [(i, i ^ 1) for i in range(parts)])
    messages = call(merge, (struct(2, 2, rows, wide),) * (chips - 1), [VMEM] * 2)(mine, swapped)
    depth_forth, lane_forth, depth_back, lane_back, half_back = call(
        matrices,
        (
            struct(VIEWS * depth, 3 * padded, dtype=BF16),
            struct(VIEWS, 2, lanes, lanes, dtype=BF16),
            struct(2, padded, VIEWS * depth, dtype=BF16),
            struct(VIEWS, 2, lanes, lanes, dtype=BF16),
            struct(padded, 3 * depth, dtype=BF16),
        ),
        [SMEM] * 5,
    )(quarter_turns, offsets, depth_taps, row_taps, column_taps)
    outer, inner = pl.pallas_call(
        pick,
        out_shape=(struct(depth, 2 * side, lanes), struct(depth, rows - 2 * side, lanes)),
        grid_spec=pltpu.PrefetchScalarGridSpec(
            num_scalar_prefetch=1,
            grid=(1,),
            in_specs=[
                pl.BlockSpec((1, depth, rows, lanes), lambda i, turns: (view_of(turns, 2), 0, 0, 0)),
                ORDER,
            ],
            out_specs=[
                pl.BlockSpec((depth, 2 * side, lanes), lambda i, turns: (0, 0, 0)),
                pl.BlockSpec((depth, rows - 2 * side, lanes), lambda i, turns: (0, 0, 0)),
            ],
        ),
        compiler_params=PARAMS,
        cost_estimate=COST,
    )(quarter_turns, recorded, messages[0])
    outer = lax.ppermute(outer, "gx", mirror)
    third, fourth = call(layers_out, (struct((rows + 2 * side) * reach, lanes),) * 2, [VMEM] * 3)(estimate, first, second)
    third, fourth = lax.ppermute(third, "gy", even_y), lax.ppermute(fourth, "gy", odd_y)
    moved = {
        k: lax.ppermute(messages[k - 1], "gx", [(i, i ^ (2 * k)) for i in range(parts)])
        for k in range(chips - 1, 0, -1)
    }

    arrivals = [half_back, *moved.values()]
    passed = call(gate, struct(8, LANES), [ORDER] * len(arrivals))(*arrivals)
    data = call(
        turned,
        struct(2, rows, depth, lanes),
        [VMEM] * (1 + chips),
        [pltpu.VMEM((parts, 2, rows, wide), F32)],
    )(mine, swapped, *[moved[k] for k in range(1, chips)])

    predicted = call(
        predict,
        struct(VIEWS, rows, depth, lanes),
        [SMEM] * 3 + [VMEM] * 7 + [ORDER],
        [
            pltpu.VMEM((rows + 2 * side, padded, lanes), F32),
            pltpu.VMEM((rows + 2 * side, VIEWS * depth, lanes), F32),
        ],
    )(quarter_turns, row_taps, column_taps, depth_forth, lane_forth, estimate, first, second, third, fourth, passed)

    inner = call(hold, struct(side * deep + 8, lanes), [VMEM] + [ORDER] * 2)(inner, predicted, outer)
    inner = lax.ppermute(inner, "gx", mirror)
    first, second, backed = call(
        project_sides,
        (struct(side, deep, lanes),) * 2 + (struct(VIEWS, 2 * side, depth, lanes),),
        [SMEM] * 3 + [VMEM] * 6,
    )(quarter_turns, row_taps, column_taps, predicted, lane_back, depth_back, kept, outer, data)
    first, second = lax.ppermute(first, "gx", even_x), lax.ppermute(second, "gx", odd_x)
    middle = call(
        project,
        struct(rows, deep, lanes),
        [SMEM] * 3 + [VMEM] * 6,
        [pltpu.VMEM((VIEWS, rows, depth, lanes), F32)],
    )(quarter_turns, row_taps, column_taps, predicted, lane_back, depth_back, kept, data, backed)
    middle = call(
        project_half,
        struct(rows, deep, lanes),
        [SMEM] * 3 + [VMEM] * 5,
        [pltpu.VMEM((rows, depth, lanes), F32), pltpu.VMEM((depth, rows - 2 * side, lanes), F32)],
    )(quarter_turns, row_taps, column_taps, predicted, lane_back, half_back, inner, middle)
    own, third, fourth = call(
        gather_sides,
        (struct(rows, depth, lanes), struct(rows * reach, lanes), struct(rows * reach, lanes)),
        [VMEM] * 3,
    )(middle, first, second)
    third, fourth = lax.ppermute(third, "gy", even_y), lax.ppermute(fourth, "gy", odd_y)
    return call(finish, struct(depth, rows, lanes), [VMEM] * 4)(estimate, own, third, fourth)


def solution(mesh):
    in_specs = (P("gy", "gx", None), P(None, "gy", "gx", None), P(), P(), P(), P(), P())
    out_specs = P("gy", "gx", None)
    return jax.shard_map(shards, mesh=mesh, in_specs=in_specs, out_specs=out_specs, check_vma=False)
```
